512 devices in a mesh: pipe: 16 (over x, y), tensor: 32 (over z, core).
Axes of the slice: x: 4, y: 4, z: 16, core: 2. Of those that a mesh axis runs over, the one named last changes fastest.
Arguments:
- hidden: bfloat16 [512, 16384], P('pipe', 'tensor'), may hold values from -18 to 18
- head_weight: bfloat16 [73728, 16384], P(('pipe', 'tensor')), may hold values from -0.703125 to 0.703125
- shares: int32 [16], replicated, may hold values from 1 to 4608, 64000 in all
- targets: int32 [512], replicated, may hold values from 0 to 63999
Outputs:
- max_logit: float32 [512], P('pipe')
- log_total: float32 [512], P('pipe')
- target_logprob: float32 [512], P('pipe')
The draws below stay inside these ranges and needn't reach their ends.
Inputs may be any that keep to these rules, and one draw needn't show every extreme that they name: Each section owns at least one word; the shares sum to 64000; some section owns exactly 4608.
All inputs are finite; a program needn't handle non-finite values.
Results may differ from the reference program's by a relative error of at most 0.0003.
Values may be sent and summed in bfloat16 or wider, within the bound.
A program may use at most 64 MiB of HBM per device.

```python
import math
import jax
import jax.numpy as jnp
import numpy as np
from jax import lax

D = 16384
CAP_DEV = 144
ROWS = 512
SECTION_CAP = 4608
COLS = 73728
VOCAB = 64000
N_PIPE = 16
N_TENSOR = 32


def base_rows(key):
    first = jax.random.fold_in(key, 0)
    third = jax.random.fold_in(key, 2)
    normal = jnp.clip(jax.random.normal(first, (ROWS, D), jnp.float32), -6.0, 6.0)
    scale = jnp.exp(jax.random.uniform(third, (ROWS,), jnp.float32, math.log(0.3), math.log(3.0)))
    return (normal, scale)


def draw_hidden(key, part):
    rows, scale = base_rows(key)
    return (rows * scale[:, None]).astype(jnp.bfloat16)


def draw_head_weight(key, part):
    key = jax.random.fold_in(key, 7)
    first, second = jax.random.split(key, 2)
    values = jnp.clip(jax.random.normal(first, (COLS, D), jnp.float32), -6.0, 6.0)
    ramp = 1.0 + 2.0 * jnp.arange(COLS, dtype=jnp.float32) / COLS
    col_scale = jnp.exp(jax.random.uniform(second, (COLS,), jnp.float32, math.log(0.5), math.log(5.0))) * ramp
    weight = values * (col_scale / math.sqrt(D))[:, None]
    return weight.astype(jnp.bfloat16)


def place_ends(drawn, key, smallest, high):
    dims = drawn.shape
    index_at = [jax.random.randint(jax.random.fold_in(key, axis), (), 0, dims[axis]) for axis in range(len(dims))]
    drawn = drawn.at[tuple(index_at)].set(smallest)
    longest = dims.index(max(dims))
    index_at[longest] = (index_at[longest] + 1) % dims[longest]
    return drawn.at[tuple(index_at)].set(high)


def profile(number_of, total, limit, lean):
    weights = [(1 << 20) // math.isqrt(grade ** lean) + 1 for grade in range(2, number_of + 1)]
    surplus, given = total - limit - (number_of - 1), [1] * (number_of - 1)
    while surplus > 0:
        free = [i for i in range(number_of - 1) if given[i] < limit]
        mass, remaining = sum([weights[i] for i in free]), surplus
        for i in free:
            addition = min(limit - given[i], max(1, remaining * weights[i] // mass), surplus)
            given[i] = given[i] + addition
            surplus = surplus - addition
    return np.array([limit] + given)


def ragged(own_key, amount, total, most, slope):
    if amount == 2:
        one = jax.random.randint(own_key, (), max(1, total - most), min(most, total - 1) + 1)
        return jnp.stack([one, total - one])
    tallies = jnp.asarray(profile(amount, total, most, slope), jnp.int32)
    couples = (amount - 1) // 2
    giver, receiver = tallies[1:1 + 2 * couples:2], tallies[2:2 + 2 * couples:2]
    slack = jnp.minimum(giver - 1, most - receiver)
    shifted = jax.random.randint(jax.random.fold_in(own_key, 1), (couples,), 0, 1 << 20) % (slack + 1)
    tallies = tallies.at[1:1 + 2 * couples:2].set(giver - shifted).at[2:2 + 2 * couples:2].set(receiver + shifted)
    return tallies[jax.random.permutation(jax.random.fold_in(own_key, 2), amount)]


def setup_inputs(seed: int = 0) -> dict:
    seeds = jax.random.split(jax.random.key(seed), 5)
    return {
        "hidden": draw_hidden(jax.random.fold_in(seeds[4], 71), 0),
        "head_weight": draw_head_weight(jax.random.fold_in(seeds[4], 71), 0),
        "shares": ragged(seeds[2], N_PIPE, VOCAB, SECTION_CAP, 2).astype(jnp.int32),
        "targets": place_ends(jax.random.randint(seeds[3], (ROWS,), 0, VOCAB), jax.random.fold_in(seeds[3], 1), 0, VOCAB - 1).astype(jnp.int32),
    }


very_negative = -1e30


def reference(hidden, head_weight, shares, targets):
    offsets = jnp.cumsum(shares) - shares
    slots = jnp.arange(SECTION_CAP, dtype=jnp.int32)
    position = (slots % CAP_DEV) * N_TENSOR + slots // CAP_DEV

    def block(section, carry):
        top, total, picked = carry
        section = jnp.asarray(section).astype(jnp.int32)
        weight = lax.dynamic_slice_in_dim(head_weight, (section * SECTION_CAP).astype(jnp.int32), SECTION_CAP, 0)
        logits = lax.dot_general(hidden, weight, (((1,), (1,)), ((), ())), preferred_element_type=jnp.float32)
        live = position < shares[section]
        word = offsets[section] + position
        local_top = jnp.max(jnp.where(live[None, :], logits, very_negative), axis=1)
        new_top = jnp.maximum(top, local_top)
        terms = jnp.where(live[None, :], jnp.exp(logits - new_top[:, None]), 0.0)
        total = total * jnp.exp(top - new_top) + jnp.sum(terms, axis=1)
        hit = live[None, :] & (word[None, :] == targets[:, None])
        picked = picked + jnp.sum(jnp.where(hit, logits, 0.0), axis=1)
        return new_top, total, picked

    start = (jnp.full((ROWS,), very_negative, jnp.float32), jnp.zeros((ROWS,), jnp.float32), jnp.zeros((ROWS,), jnp.float32))
    top, total, picked = lax.fori_loop(0, N_PIPE, block, start)
    log_total = top + jnp.log(total)
    return top, log_total, picked - log_total
```

```python
import jax
import jax.numpy as jnp
from jax import lax
from jax.experimental import pallas as pl
from jax.experimental.pallas import tpu as pltpu
from jax.sharding import PartitionSpec as P

VERY_NEGATIVE = -1e30
NX, NY, NZ, NQ = 4, 4, 16, 4
ROWS = 32
WIDTH = 512
WIDE = 384
HALF = 16
SLOTS = 144
MESH = pl.DeviceIdType.MESH


def combine(tiles):
    tops = [t[0:1, :] for t in tiles]
    top = tops[0]
    for other in tops[1:]:
        top = jnp.maximum(top, other)
    total = jnp.zeros_like(top)
    pick = jnp.zeros_like(top)
    for t, own in zip(tiles, tops):
        total = total + t[1:2, :] * jnp.exp(own - top)
        pick = pick + t[2:3, :]
    return top, total, pick


def kernel(hidden, weight, shares, targets, top_out, log_out, pick_out,
           X, W, acc, part, st, sx, sy, sz1, sz2, sc,
           a1s, a1r, a2s, a2r, z1s, z1r, z2s, z2r, us, ur, vs, vr, fs, fr, rs, rr,
           ws, wr, wl, hl, ps, pr, ss, sr):
    pipe = lax.axis_index("pipe")
    tensor = lax.axis_index("tensor")
    x, y = pipe // NY, pipe % NY
    z, c = tensor // 2, tensor % 2
    zq, zr = z // NQ, z % NQ

    def at_x(d):
        return (((x + d) % NX) * NY + y, tensor)

    def at_y(d):
        return (x * NY + (y + d) % NY, tensor)

    def at_z(d):
        return (pipe, ((z + d) % NZ) * 2 + c)

    sibling = (pipe, z * 2 + 1 - c)

    def send(src, dst, send_sem, recv_sem, device):
        copy = pltpu.make_async_remote_copy(
            src_ref=src, dst_ref=dst, send_sem=send_sem, recv_sem=recv_sem,
            device_id=device, device_id_type=MESH)
        copy.start()
        sent.append(copy)

    sent = []

    def arrived(ref, sem):
        pltpu.make_async_copy(ref, ref, sem).wait()

    own_block = pltpu.make_async_copy(hidden, X.at[zq, zr, x, y], hl)
    own_block.start()

    def own_weight(k):
        col = pl.multiple_of((2 * k + c) * WIDTH, WIDTH)
        return pltpu.make_async_copy(
            weight.at[:, pl.ds(col, WIDTH)], W.at[k, pl.ds(0, SLOTS), :], wl.at[k])

    def other_weight(k):
        col = pl.multiple_of((2 * k + 1 - c) * WIDTH, WIDTH)
        return pltpu.make_async_remote_copy(
            src_ref=weight.at[:, pl.ds(col, WIDTH)],
            dst_ref=W.at[k, pl.ds(SLOTS, SLOTS), :],
            send_sem=ws.at[k], recv_sem=wr.at[k], device_id=sibling, device_id_type=MESH)

    barrier = pltpu.get_barrier_semaphore()
    greet = [at_x(1), at_x(2), at_x(3), at_y(1), at_y(2), at_y(3), sibling]
    greet += [at_z(d) for d in (1, 2, 4, 8, 12, 14, 15)]
    for device in greet:
        pl.semaphore_signal(barrier, inc=1, device_id=device, device_id_type=MESH)
    pl.semaphore_wait(barrier, len(greet))

    mine = X.at[zq, zr, x, y]
    for i, d in enumerate((4, 12, 8)):
        send(hidden.at[:, pl.ds(0, WIDE)], mine.at[:, pl.ds(0, WIDE)],
             z1s.at[i], z1r.at[i], at_z(d))
    for i, d in enumerate((1, 3, 2)):
        send(hidden.at[:, pl.ds(WIDE, WIDTH - WIDE)], mine.at[:, pl.ds(WIDE, WIDTH - WIDE)],
             a1s.at[i], a1r.at[i], at_x(d))

    @pl.loop(0, NZ)
    def _(k):
        other_weight(k).start()

    @pl.loop(0, NZ)
    def _(k):
        own_weight(k).start()

    own_block.wait()
    for i in range(3):
        arrived(X.at[zq, zr, x, y, :, pl.ds(WIDE, WIDTH - WIDE)], a1r.at[i])
    line = X.at[zq, zr, :, y, :, pl.ds(WIDE, WIDTH - WIDE)]
    for i, d in enumerate((1, 3, 2)):
        send(line, line, a2s.at[i], a2r.at[i], at_y(d))

    for i in range(3):
        arrived(mine.at[:, pl.ds(0, WIDE)], z1r.at[i])
    line = X.at[:, zr, x, y, :, pl.ds(0, WIDE)]
    for i, d in enumerate((1, 15, 2)):
        send(line, line, z2s.at[i], z2r.at[i], at_z(d))

    for i in range(3):
        arrived(X.at[zq, zr, :, y, :, pl.ds(WIDE, WIDTH - WIDE)], a2r.at[i])

    def slab(d, begin, count):
        at = (z + d) % NZ
        return X.at[at // NQ, at % NQ, pl.ds(begin, count), :, :, pl.ds(WIDE, WIDTH - WIDE)]

    def ring(step):
        begin, count = ((0, 4), (0, 4)) if step < 7 else ((0, 2), (2, 2))
        if step == 7:
            begin, count = (0, 2), (2, 2)
        else:
            begin, count = (0, 0), (4, 4)
        up, down = slab(NZ - step, begin[0], count[0]), slab(step, begin[1], count[1])
        send(up, up, rs.at[0, step], rr.at[0, step], at_z(1))
        send(down, down, rs.at[1, step], rr.at[1, step], at_z(15))

    def ring_wait(step):
        if step == 7:
            begin, count = (0, 2), (2, 2)
        else:
            begin, count = (0, 0), (4, 4)
        arrived(slab(NZ - step - 1, begin[0], count[0]), rr.at[0, step])
        arrived(slab(step + 1, begin[1], count[1]), rr.at[1, step])

    ring(0)

    for i in range(3):
        arrived(X.at[:, zr, x, y, :, pl.ds(0, WIDE)], z2r.at[i])

    def column(part_id, du, dv, q0=0, nq=NQ):
        cx, cy = ((x + du) % NX, (y + dv) % NY) if part_id == 0 else ((x + dv) % NX, (y + du) % NY)
        return X.at[pl.ds(q0, nq), :, cx, cy, pl.ds(part_id * HALF, HALF), pl.ds(0, WIDE)]

    def along_u(part_id, d):
        return at_x(d) if part_id == 0 else at_y(d)

    def along_v(part_id, d):
        return at_y(d) if part_id == 0 else at_x(d)

    hops = (0, 3, 1, 2)

    def direct(k):
        for q in range(2):
            block = column(q, hops[k], 0)
            for i, d in enumerate((1, 3)):
                send(block, block, vs.at[q, k, i], vr.at[q, k, i], along_v(q, d))

    def forward(k):
        for q in range(2):
            arrived(column(q, hops[k], 3), vr.at[q, k, 0])
            block = column(q, hops[k], 3, 0, 2)
            send(block, block, fs.at[q, k, 0], fr.at[q, k, 0], along_v(q, 1))
            arrived(column(q, hops[k], 1), vr.at[q, k, 1])
            block = column(q, hops[k], 1, 2, 2)
            send(block, block, fs.at[q, k, 1], fr.at[q, k, 1], along_v(q, 3))

    for q in range(2):
        block = column(q, 0, 0)
        for i, d in enumerate((1, 3, 2)):
            send(block, block, us.at[q, i], ur.at[q, i], along_u(q, d))
    direct(0)

    def u_wait(k):
        for q in range(2):
            arrived(column(q, hops[k], 0), ur.at[q, k - 1])

    ring_wait(0)
    ring(1)
    u_wait(1)
    direct(1)
    ring_wait(1)
    ring(2)
    u_wait(2)
    direct(2)
    ring_wait(2)
    ring(3)
    u_wait(3)
    direct(3)
    ring_wait(3)
    ring(4)
    forward(0)
    ring_wait(4)
    ring(5)
    forward(1)
    ring_wait(5)
    ring(6)
    forward(2)
    ring_wait(6)
    ring(7)
    forward(3)
    ring_wait(7)
    for k in range(4):
        for q in range(2):
            arrived(column(q, hops[k], 2, 0, 2), fr.at[q, k, 0])
            arrived(column(q, hops[k], 2, 2, 2), fr.at[q, k, 1])

    @pl.loop(0, NZ)
    def _(k):
        own_weight(k).wait()
        other_weight(k).wait()

    acc[...] = jnp.zeros_like(acc)

    @pl.loop(0, NZ)
    def _(k):
        rows = X[k // NQ, k % NQ].reshape(NX * NY * ROWS, WIDTH)
        acc[...] += lax.dot_general(
            W[k], rows, (((1,), (1,)), ((), ())), preferred_element_type=jnp.float32)

    swap = pltpu.make_async_remote_copy(
        src_ref=acc.at[pl.ds(SLOTS, SLOTS), :], dst_ref=part, send_sem=ps, recv_sem=pr,
        device_id=sibling, device_id_type=MESH)
    swap.start()

    own_share = jnp.int32(0)
    offset = jnp.int32(0)
    for s in range(NX * NY):
        own_share = own_share + jnp.where(s == pipe, shares[s], 0)
        offset = offset + jnp.where(s < pipe, shares[s], 0)
    position = lax.broadcasted_iota(jnp.int32, (SLOTS, NX * NY * ROWS), 0) * (2 * NZ) + tensor
    live = position < own_share
    hit = live & (position + offset == targets[...])
    swap.wait()
    logits = acc[pl.ds(0, SLOTS), :] + part[...]
    top = jnp.max(jnp.where(live, logits, VERY_NEGATIVE), axis=0, keepdims=True)
    total = jnp.sum(jnp.where(live, jnp.exp(logits - top), 0.0), axis=0, keepdims=True)
    pick = jnp.sum(jnp.where(hit, logits, 0.0), axis=0, keepdims=True)

    def put(ref, values):
        for i, v in enumerate(values):
            ref[pl.ds(i, 1), :] = v

    st[...] = jnp.zeros_like(st)
    for k in range(NX):
        for i, v in enumerate((top, total, pick)):
            st[k, pl.ds(i, 1), :] = v[:, 128 * k:128 * (k + 1)]

    for i, d in enumerate((1, 3, 2)):
        send(st.at[(x + d) % NX], sx.at[x], ss.at[0, i], sr.at[0, i], at_x(d))
    sx[x] = st[x]
    for i in range(3):
        arrived(sx.at[0], sr.at[0, i])

    def stage(n, here, buf, me, peers):
        buf[me] = jnp.zeros((8, 128), jnp.float32)
        put(buf.at[me], here)
        for i, device in enumerate(peers):
            send(buf.at[me], buf.at[me], ss.at[n, i], sr.at[n, i], device)
        for i in range(len(peers)):
            arrived(buf.at[0], sr.at[n, i])
        return combine([buf[i] for i in range(buf.shape[0])])

    here = combine([sx[i] for i in range(NX)])
    here = stage(1, here, sy, y, [at_y(1), at_y(3), at_y(2)])
    here = stage(2, here, sz1, zq, [at_z(4), at_z(12), at_z(8)])
    here = stage(3, here, sz2, zr, [at_z(1), at_z(15), at_z(2)])
    top, total, pick = stage(4, here, sc, c, [sibling])
    log_total = top + jnp.log(total)
    for out, v in ((top_out, top), (log_out, log_total), (pick_out, pick - log_total)):
        own = jnp.zeros((1, ROWS), jnp.float32)
        for k in range(NY):
            own = jnp.where(y == k, v[:, ROWS * k:ROWS * (k + 1)], own)
        out[...] = own
    for copy in sent:
        copy.wait_send()


def local(hidden, head_weight, shares, targets):
    dma = pltpu.SemaphoreType.DMA
    rows = NX * NY * ROWS
    tile = lambda n: pltpu.VMEM((n, 8, 128), jnp.float32)
    pairs = [(3,), (3,), (3,), (3,), (2, 3), (2, 4, 2), (2, 4, 2), (2, 8)]
    sems = [dma(s) for s in pairs for _ in range(2)]
    outs = pl.pallas_call(
        kernel,
        out_shape=[jax.ShapeDtypeStruct((1, ROWS), jnp.float32)] * 3,
        in_specs=[
            pl.BlockSpec(memory_space=pl.ANY),
            pl.BlockSpec(memory_space=pl.ANY),
            pl.BlockSpec(memory_space=pltpu.SMEM),
            pl.BlockSpec(memory_space=pltpu.VMEM),
        ],
        out_specs=[pl.BlockSpec(memory_space=pltpu.VMEM)] * 3,
        scratch_shapes=[
            pltpu.VMEM((NQ, NZ // NQ, NX, NY, ROWS, WIDTH), jnp.bfloat16),
            pltpu.VMEM((NZ, 2 * SLOTS, WIDTH), jnp.bfloat16),
            pltpu.VMEM((2 * SLOTS, rows), jnp.float32),
            pltpu.VMEM((SLOTS, rows), jnp.float32),
            tile(NX), tile(NX), tile(NY), tile(NQ), tile(NQ), tile(2),
            *sems,
            dma((NZ,)), dma((NZ,)), dma((NZ,)), dma(()), dma(()), dma(()),
            dma((5, 3)), dma((5, 3)),
        ],
        compiler_params=pltpu.CompilerParams(
            collective_id=0, has_side_effects=True, vmem_limit_bytes=48 * 1024 * 1024),
        cost_estimate=pl.CostEstimate(
            flops=2 * rows * SLOTS * 2 * NZ * WIDTH, bytes_accessed=22 * 1024 * 1024,
            transcendentals=rows * SLOTS),
    )(hidden, head_weight, shares, targets.reshape(1, rows))
    return tuple(o.reshape(ROWS) for o in outs)


def solution(mesh):
    in_specs = (P("pipe", "tensor"), P(("pipe", "tensor"), None), P(), P())
    out_specs = (P("pipe"), P("pipe"), P("pipe"))
    return jax.shard_map(local, mesh=mesh, in_specs=in_specs, out_specs=out_specs, check_vma=False)
```

```python
import jax
import jax.numpy as jnp
from jax import lax
from jax.experimental import pallas as pl
from jax.experimental.pallas import tpu as pltpu
from jax.sharding import PartitionSpec as P

VERY_NEGATIVE = -1e30
NX, NY, NZ = 4, 4, 16
FAR = NZ // 2
ROWS = 32
HALF = 16
WIDTH = 512
WIDE = 384
SLOTS = 144
LANES = 128
MESH = pl.DeviceIdType.MESH
TIMES = dict(z=2.8, o=3.2, v=4.1, v0=6.0, a0=6.5, a=3.4, m=4.2)


def below(s):
    return 2 * s - 1 if s else 0


def above(s):
    return 2 * s


def pair(s):
    if s == 0:
        return 0, 1
    return (2 * s - 1, 2) if s < FAR else (2 * FAR - 1, 1)


def join(v):
    lane = lax.broadcasted_iota(jnp.int32, (1, LANES), 1)
    middle = (lane >= ROWS) & (lane < 2 * ROWS)
    rows = [v[i] for i in range(v.shape[0])]
    top = rows[0]
    for r in rows[1:]:
        top = jnp.maximum(top, r)
    total = jnp.zeros_like(top)
    for r in rows:
        scale = pltpu.roll(jnp.exp(r - top), ROWS, 1)
        total = total + r * jnp.where(middle, scale, 1.0)
    return jnp.where(lane < ROWS, top, total)


def kernel(hidden, weight, shares, targets, out,
           X, W, acc, part, goal, own_sh, pack, sxy, sz, sc,
           zs, zr, a1s, a1r, a2s, a2r, rs, rr, os, orr, vs, vr, fs, fr,
           ws, wr, wl, hl, gl, ps, pr, xs, xr, ts, tr, cs, cr):
    pipe = lax.axis_index("pipe")
    tensor = lax.axis_index("tensor")
    x, y = pipe // NY, pipe % NY
    z, c = tensor // 2, tensor % 2

    def at_xy(dx, dy):
        return (((x + dx) % NX) * NY + (y + dy) % NY, tensor)

    def at_z(d):
        return (pipe, ((z + d) % NZ) * 2 + c)

    sibling = (pipe, z * 2 + 1 - c)
    sent = []

    def send(src, dst, send_sem, recv_sem, device):
        copy = pltpu.make_async_remote_copy(
            src_ref=src, dst_ref=dst, send_sem=send_sem, recv_sem=recv_sem,
            device_id=device, device_id_type=MESH)
        copy.start()
        sent.append(copy)

    def arrived(ref, sem):
        pltpu.make_async_copy(ref, ref, sem).wait()

    def feature_block(j, core):
        step = (j + 1) // 2
        at = jnp.where(j % 2 == 1, z + NZ - step, z + step) % NZ
        return pl.ds(pl.multiple_of((2 * at + core) * WIDTH, WIDTH), WIDTH)

    def own_weight(j):
        return pltpu.make_async_copy(
            weight.at[:, feature_block(j, c)], W.at[j, pl.ds(0, SLOTS), :], wl.at[j])

    def other_weight(j):
        return pltpu.make_async_remote_copy(
            src_ref=weight.at[:, feature_block(j, 1 - c)],
            dst_ref=W.at[j, pl.ds(SLOTS, SLOTS), :],
            send_sem=ws.at[j], recv_sem=wr.at[j], device_id=sibling, device_id_type=MESH)

    barrier = pltpu.get_barrier_semaphore()
    greet = [at_xy(1, 0), at_xy(3, 0), at_xy(0, 1), at_xy(0, 3), at_z(1), at_z(15),
             at_xy(2, 0), at_xy(0, 2), sibling]
    for device in greet:
        pl.semaphore_signal(barrier, inc=1, device_id=device, device_id_type=MESH)
    own_block = pltpu.make_async_copy(hidden, X.at[0, 0, 0], hl)
    own_block.start()
    pl.semaphore_wait(barrier, len(greet))

    wide, narrow = pl.ds(0, WIDE), pl.ds(WIDE, WIDTH - WIDE)
    upper, lower = pl.ds(0, HALF), pl.ds(HALF, HALF)
    both = pl.ds(0, ROWS)

    def z_send(s):
        src_up = hidden.at[:, wide] if s == 1 else X.at[below(s - 1), 0, 0, :, wide]
        src_down = hidden.at[:, wide] if s == 1 else X.at[above(s - 1), 0, 0, :, wide]
        dst_up, dst_down = X.at[below(s), 0, 0, :, wide], X.at[min(above(s), NZ - 1), 0, 0, :, wide]
        if s == FAR:
            src_up, dst_up = src_up.at[upper], dst_up.at[upper]
            src_down, dst_down = src_down.at[lower], dst_down.at[lower]
        send(src_up, dst_up, zs.at[s - 1, 0], zr.at[s - 1, 0], at_z(1))
        send(src_down, dst_down, zs.at[s - 1, 1], zr.at[s - 1, 1], at_z(15))

    def z_wait(s):
        a, b = X.at[below(s), 0, 0, :, wide], X.at[min(above(s), NZ - 1), 0, 0, :, wide]
        if s == FAR:
            a, b = a.at[upper], b.at[lower]
        arrived(a, zr.at[s - 1, 0])
        arrived(b, zr.at[s - 1, 1])

    def o_send(s):
        first, n = pair(s)
        at = pl.ds(first, n)
        if s == 0:
            def src(r):
                return hidden.at[r, wide]

            def dst(a, b, r):
                return X.at[0, a, b, r, wide]
        else:
            def src(r):
                return X.at[at, 0, 0, r, wide]

            def dst(a, b, r):
                return X.at[at, a, b, r, wide]
        plan = [((1, 0), both), ((0, 1), both), ((3, 0), both), ((0, 3), both), ((2, 0), upper), ((0, 2), lower)]
        for i, ((dx, dy), r) in enumerate(plan):
            send(src(r), dst(-dx % NX, -dy % NY, r), os.at[s, i], orr.at[s, i], at_xy(dx, dy))

    def o_wait(s):
        at = pl.ds(*pair(s))
        plan = [((1, 0), both), ((0, 1), both), ((3, 0), both), ((0, 3), both), ((2, 0), upper), ((0, 2), lower)]
        for i, ((dx, dy), r) in enumerate(plan):
            arrived(X.at[at, -dx % NX, -dy % NY, r, wide], orr.at[s, i])

    def v_send(s):
        at, rest = pl.ds(*pair(s)), pl.ds(1, 3)
        for i, d in enumerate((1, 3)):
            send(X.at[at, rest, 0, upper, wide], X.at[at, rest, -d % NY, upper, wide],
                 vs.at[s, 0, i], vr.at[s, 0, i], at_xy(0, d))
            send(X.at[at, 0, rest, lower, wide], X.at[at, -d % NX, rest, lower, wide],
                 vs.at[s, 1, i], vr.at[s, 1, i], at_xy(d, 0))

    def v_wait(s):
        at, rest = pl.ds(*pair(s)), pl.ds(1, 3)
        for i, d in enumerate((1, 3)):
            arrived(X.at[at, rest, -d % NY, upper, wide], vr.at[s, 0, i])
            arrived(X.at[at, -d % NX, rest, lower, wide], vr.at[s, 1, i])

    def f_send(s):
        at = pl.ds(*pair(s))
        for i, d in enumerate((1, 3)):
            h = pl.ds(2 * i, 2)
            send(X.at[at, h, -d % NY, upper, wide], X.at[at, h, 2, upper, wide],
                 fs.at[s, 0, i], fr.at[s, 0, i], at_xy(0, d))
            send(X.at[at, -d % NX, h, lower, wide], X.at[at, 2, h, lower, wide],
                 fs.at[s, 1, i], fr.at[s, 1, i], at_xy(d, 0))

    def f_wait(s):
        at = pl.ds(*pair(s))
        for i in range(2):
            h = pl.ds(2 * i, 2)
            arrived(X.at[at, h, 2, upper, wide], fr.at[s, 0, i])
            arrived(X.at[at, 2, h, lower, wide], fr.at[s, 1, i])

    def a1_send():
        for i, d in enumerate((1, 3, 2)):
            send(hidden.at[:, narrow], X.at[0, -d % NX, 0, :, narrow], a1s.at[i], a1r.at[i], at_xy(d, 0))

    def a2_send():
        for i, d in enumerate((1, 3, 2)):
            arrived(X.at[0, -d % NX, 0, :, narrow], a1r.at[i])
        for i, d in enumerate((1, 3, 2)):
            send(X.at[0, :, 0, :, narrow], X.at[0, :, -d % NY, :, narrow], a2s.at[i], a2r.at[i], at_xy(0, d))

    def a2_wait():
        for i, d in enumerate((1, 3, 2)):
            arrived(X.at[0, :, -d % NY, :, narrow], a2r.at[i])

    def slab(j, h):
        return X.at[j, pl.ds(2 * h, 2), :, :, narrow]

    def ring_send(s, h):
        if s < FAR or h == 0:
            send(slab(below(s - 1), h), slab(below(s), h), rs.at[s - 1, h, 0], rr.at[s - 1, h, 0], at_z(1))
        if s < FAR or h == 1:
            send(slab(above(s - 1), h), slab(min(above(s), NZ - 1), h),
                 rs.at[s - 1, h, 1], rr.at[s - 1, h, 1], at_z(15))

    def ring_wait(s, h):
        if s < FAR or h == 0:
            arrived(slab(below(s), h), rr.at[s - 1, h, 0])
        if s < FAR or h == 1:
            arrived(slab(min(above(s), NZ - 1), h), rr.at[s - 1, h, 1])

    def multiply(s):
        first, n = pair(s)
        for j in range(first, first + n):
            own_weight(j).wait()
            other_weight(j).wait()
        @pl.loop(first, first + n)
        def _(j):
            part_sum = lax.dot_general(
                W[j], X[j].reshape(NX * NY * ROWS, WIDTH),
                (((1,), (1,)), ((), ())), preferred_element_type=jnp.float32)
            if s == 0:
                acc[...] = part_sum
            else:
                acc[...] += part_sum

    events = []

    def add(time, *steps):
        events.append((time, len(events), steps))

    T = TIMES
    z_send(1)
    o_send(0)
    a1_send()

    @pl.loop(0, NZ)
    def _(j):
        other_weight(j).start()
        own_weight(j).start()

    own_block.wait()
    goals = [pltpu.make_async_copy(targets.at[(x + d) % NX], goal.at[d], gl.at[d]) for d in range(NX)]
    share_copy = pltpu.make_async_copy(shares, own_sh, gl.at[NX])
    for g in goals + [share_copy]:
        g.start()

    ring_at = {s: T['a0'] + T['a'] * s for s in range(FAR + 1)}
    add(3.0, a2_send)
    add(T['a0'], a2_wait, lambda: ring_send(1, 0), lambda: ring_send(1, 1))
    for s in range(1, FAR + 1):
        for h in range(2):
            steps = [lambda s=s, h=h: ring_wait(s, h)]
            if s < FAR:
                steps.append(lambda s=s, h=h: ring_send(s + 1, h))
            add(ring_at[s] + (T['a'] / 2) * (h - 1), *steps)
    v_last = 0.0
    for s in range(FAR + 1):
        z_at = T['z'] * s
        if s:
            steps = [lambda s=s: z_wait(s)]
            if s < FAR:
                steps.append(lambda s=s: z_send(s + 1))
            steps.append(lambda s=s: o_send(s))
            add(z_at, *steps)
        o_at = z_at + T['o']
        add(o_at, lambda s=s: o_wait(s), lambda s=s: v_send(s))
        v_at = max(o_at + 2.5, T['v0'] + T['v'] * s)
        add(v_at, lambda s=s: v_wait(s), lambda s=s: f_send(s))
        add(max(v_at + T['m'], ring_at[s] + 0.01), lambda s=s: f_wait(s), lambda s=s: multiply(s))
    for _, _, steps in sorted(events, key=lambda e: e[:2]):
        for step in steps:
            step()

    swap = pltpu.make_async_remote_copy(
        src_ref=acc.at[pl.ds(SLOTS, SLOTS), :], dst_ref=part, send_sem=ps, recv_sem=pr,
        device_id=sibling, device_id_type=MESH)
    swap.start()
    for g in goals + [share_copy]:
        g.wait()
    own_share = jnp.int32(0)
    offset = jnp.int32(0)
    for s in range(NX * NY):
        own_share = own_share + jnp.where(s == pipe, own_sh[s], 0)
        offset = offset + jnp.where(s < pipe, own_sh[s], 0)
    position = lax.broadcasted_iota(jnp.int32, (SLOTS, 1), 0) * (2 * NZ) + tensor
    live = position < own_share
    word = position + offset
    lane = lax.broadcasted_iota(jnp.int32, (1, LANES), 1)
    swap.wait()

    def packed(values, dy):
        top, total, pick = values
        moved = [pltpu.roll(v, (ROWS * (i - dy)) % LANES, 1) if (ROWS * (i - dy)) % LANES else v
                 for i, v in enumerate((top, total, pick))]
        return jnp.where(lane < ROWS, moved[0], jnp.where(lane < 2 * ROWS, moved[1], moved[2]))

    for dx in range(NX):
        cols = pl.ds(dx * LANES, LANES)
        logits = acc[pl.ds(0, SLOTS), cols] + part[:, cols]
        want = goal[dx]
        turned = want
        for k in range(1, NY):
            turned = jnp.where(y == k, pltpu.roll(want, LANES - ROWS * k, 1), turned)
        top = jnp.max(jnp.where(live, logits, VERY_NEGATIVE), axis=0, keepdims=True)
        total = jnp.sum(jnp.where(live, jnp.exp(logits - top), 0.0), axis=0, keepdims=True)
        pick = jnp.sum(jnp.where(live & (word == turned), logits, 0.0), axis=0, keepdims=True)
        for dy in range(NY):
            row = packed((top, total, pick), dy)
            if dx == 0 and dy == 0:
                sxy[0] = row
            else:
                pack[dx * NY + dy] = row
                to = (-dx % NX) * NY + (-dy % NY)
                send(pack.at[dx * NY + dy], sxy.at[to], xs.at[to], xr.at[to], at_xy(dx, dy))
    for i in range(1, NX * NY):
        arrived(sxy.at[i], xr.at[i])
    sz[z] = join(sxy[...])
    for d in (8, 7, 9, 6, 10, 5, 11, 4, 12, 3, 13, 2, 14, 1, 15):
        send(sz.at[z], sz.at[z], ts.at[d], tr.at[d], at_z(d))
    while len(sent) > 15:
        sent.pop(0).wait_send()
    for d in range(1, NZ):
        arrived(sz.at[(z + NZ - d) % NZ], tr.at[d])
    sc[c] = join(sz[...])
    send(sc.at[c], sc.at[c], cs, cr, sibling)
    arrived(sc.at[1 - c], cr)
    row = join(sc[...])
    log_total = pltpu.roll(row, ROWS, 1) + jnp.log(jnp.where((lane >= ROWS) & (lane < 2 * ROWS), row, 1.0))
    out[...] = jnp.where(lane < ROWS, row, jnp.where(
        lane < 2 * ROWS, log_total, row - pltpu.roll(log_total, ROWS, 1)))
    for copy in sent:
        copy.wait_send()


def local(hidden, head_weight, shares, targets):
    dma = pltpu.SemaphoreType.DMA
    rows = NX * NY * ROWS
    n = FAR + 1
    line = lambda k: pltpu.VMEM((k, 1, LANES), jnp.float32)
    pairs = [(FAR, 2), (3,), (3,), (FAR, 2, 2), (n, 6), (n, 2, 2), (n, 2, 2)]
    hbm = pl.BlockSpec(memory_space=pltpu.HBM)
    out = pl.pallas_call(
        kernel,
        out_shape=jax.ShapeDtypeStruct((1, LANES), jnp.float32),
        in_specs=[hbm] * 4,
        out_specs=pl.BlockSpec(memory_space=pltpu.VMEM),
        scratch_shapes=[
            pltpu.VMEM((NZ, NX, NY, ROWS, WIDTH), jnp.bfloat16),
            pltpu.VMEM((NZ, 2 * SLOTS, WIDTH), jnp.bfloat16),
            pltpu.VMEM((2 * SLOTS, rows), jnp.float32),
            pltpu.VMEM((SLOTS, rows), jnp.float32),
            pltpu.VMEM((NX, 1, LANES), jnp.int32),
            pltpu.SMEM((NX * NY,), jnp.int32),
            line(16), line(16), line(NZ), line(2),
            *[dma(s) for s in pairs for _ in range(2)],
            dma((NZ,)), dma((NZ,)), dma((NZ,)), dma(()), dma((NX + 1,)), dma(()), dma(()),
            dma((16,)), dma((16,)), dma((NZ,)), dma((NZ,)), dma(()), dma(()),
        ],
        compiler_params=pltpu.CompilerParams(
            collective_id=0, has_side_effects=True, vmem_limit_bytes=60 * 1024 * 1024),
        cost_estimate=pl.CostEstimate(
            flops=2 * rows * SLOTS * 2 * NZ * WIDTH, bytes_accessed=22 * 1024 * 1024,
            transcendentals=rows * SLOTS),
    )(hidden, head_weight, shares, targets.reshape(NX, 1, LANES))
    return tuple(out[0, ROWS * i:ROWS * (i + 1)] for i in range(3))


def solution(mesh):
    in_specs = (P("pipe", "tensor"), P(("pipe", "tensor"), None), P(), P())
    out_specs = (P("pipe"), P("pipe"), P("pipe"))
    return jax.shard_map(local, mesh=mesh, in_specs=in_specs, out_specs=out_specs, check_vma=False)
```

```python
import math

import jax
import jax.numpy as jnp
from jax import lax
from jax.experimental import pallas as pl
from jax.experimental.pallas import tpu as pltpu
from jax.sharding import PartitionSpec as P

VERY_NEGATIVE = -1e30
NX, NY, NZ = 4, 4, 16
FAR = NZ // 2
ROWS = 32
HALF = 16
WIDTH = 512
WIDE = 384
SLOTS = 144
LANES = 128
MESH = pl.DeviceIdType.MESH
HOP = (1, 1, 1, 1, 1, 1, 1, 1)
PIECES = 8
ORDER = (
    ("z", 1), ("a2",), ("a0",), ("o", 0), ("z", 2), ("r", 1, 1), ("r", 1, 0), ("o", 1), ("z", 3), ("a3",),
    ("v", 0), ("r", 2, 1), ("r", 2, 0), ("o", 2), ("z", 4), ("m", 0), ("r", 1, 5), ("r", 1, 7), ("r", 1, 3),
    ("r", 1, 2), ("r", 1, 4), ("r", 1, 6), ("r", 3, 1), ("r", 3, 0), ("o", 3), ("v", 1), ("z", 5), ("v", 2),
    ("o", 4), ("r", 2, 5), ("r", 2, 7), ("r", 2, 3), ("r", 2, 2), ("r", 2, 4), ("r", 2, 6), ("r", 4, 1), ("r",
    4, 0), ("z", 6), ("r", 3, 5), ("r", 3, 7), ("r", 3, 3), ("m", 1), ("r", 3, 2), ("o", 5), ("r", 3, 4),
    ("v", 3), ("r", 3, 6), ("r", 5, 1), ("r", 5, 0), ("r", 4, 5), ("z", 7), ("r", 4, 7), ("r", 4, 3), ("m",
    2), ("o", 6), ("v", 4), ("r", 4, 2), ("r", 4, 4), ("r", 4, 6), ("r", 6, 1), ("r", 6, 0), ("z", 8), ("r",
    5, 5), ("r", 5, 7), ("r", 5, 3), ("r", 5, 2), ("r", 5, 4), ("m", 3), ("r", 5, 6), ("v", 5), ("r", 7, 1),
    ("o", 7), ("r", 7, 0), ("r", 6, 5), ("r", 6, 7), ("r", 6, 3), ("o", 8), ("r", 6, 2), ("r", 6, 4), ("m",
    4), ("v", 6), ("r", 6, 6), ("r", 8, 1), ("r", 8, 0), ("m", 5), ("r", 7, 5), ("r", 7, 7), ("r", 7, 3),
    ("v", 7), ("r", 7, 2), ("r", 7, 4), ("v", 8), ("r", 7, 6), ("m", 6), ("r", 8, 5), ("r", 8, 7), ("r", 8,
    3), ("r", 8, 2), ("r", 8, 4), ("r", 8, 6), ("m", 8), ("m", 7),
)
DXS = (2, 1, 3, 0)


def below(s):
    return 2 * s - 1 if s else 0


def above(s):
    return 2 * s


def pair(s):
    if s == 0:
        return 0, 1
    return (2 * s - 1, 2) if s < FAR else (2 * FAR - 1, 1)


def join(v):
    lane = lax.broadcasted_iota(jnp.int32, (1, LANES), 1)
    middle = (lane >= ROWS) & (lane < 2 * ROWS)
    rows = [v[i] for i in range(v.shape[0])]
    top = rows[0]
    for r in rows[1:]:
        top = jnp.maximum(top, r)
    total = jnp.zeros_like(top)
    for r in rows:
        scale = pltpu.roll(jnp.exp(r - top), ROWS, 1)
        total = total + r * jnp.where(middle, scale, 1.0)
    return jnp.where(lane < ROWS, top, total)


def kernel(hidden, weight, shares, targets, out,
           X, W, acc, part, spare, goal, own_sh, pack, sxy, sz, sc,
           out_sem, zr, ar, rr, orr, vr, fr, ws, wr, wl, hl, gl, ps, pr,
           xs, xr, ts, tr, cs, cr):
    pipe = lax.axis_index("pipe")
    tensor = lax.axis_index("tensor")
    x, y = pipe // NY, pipe % NY
    z, c = tensor // 2, tensor % 2

    def at_xy(dx, dy):
        return (((x + dx) % NX) * NY + (y + dy) % NY, tensor)

    def at_z(d):
        return (pipe, ((z + d) % NZ) * 2 + c)

    sibling = (pipe, z * 2 + 1 - c)
    sent = []

    def send(src, dst, recv_sem, device):
        pltpu.make_async_remote_copy(
            src_ref=src, dst_ref=dst, send_sem=out_sem, recv_sem=recv_sem,
            device_id=device, device_id_type=MESH).start()
        sent.append(math.prod(src.shape))

    def arrived(ref, sem):
        pltpu.make_async_copy(ref, ref, sem).wait()

    def feature_block(j, core):
        step = (j + 1) // 2
        at = jnp.where(j % 2 == 1, z + NZ - step, z + step) % NZ
        return pl.ds(pl.multiple_of((2 * at + core) * WIDTH, WIDTH), WIDTH)

    def own_weight(j):
        return pltpu.make_async_copy(
            weight.at[:, feature_block(j, c)], W.at[j, pl.ds(0, SLOTS), :], wl)

    def other_weight(j):
        return pltpu.make_async_remote_copy(
            src_ref=weight.at[:, feature_block(j, 1 - c)],
            dst_ref=W.at[j, pl.ds(SLOTS, SLOTS), :],
            send_sem=ws, recv_sem=wr, device_id=sibling, device_id_type=MESH)

    barrier = pltpu.get_barrier_semaphore()
    greet = [at_xy(1, 0), at_xy(3, 0), at_xy(0, 1), at_xy(0, 3), at_z(1), at_z(15),
             at_xy(2, 0), at_xy(0, 2), sibling]
    for device in greet:
        pl.semaphore_signal(barrier, inc=1, device_id=device, device_id_type=MESH)
    own_block = pltpu.make_async_copy(hidden, X.at[0, 0, 0], hl)
    own_block.start()
    pl.semaphore_wait(barrier, len(greet))

    wide, narrow = pl.ds(0, WIDE), pl.ds(WIDE, WIDTH - WIDE)
    upper, lower = pl.ds(0, HALF), pl.ds(HALF, HALF)
    both = pl.ds(0, ROWS)

    def z_send(s):
        hop = HOP[s - 1]
        if s == hop:
            src_up = src_down = hidden.at[:, wide]
        else:
            src_up, src_down = X.at[below(s - hop), 0, 0, :, wide], X.at[above(s - hop), 0, 0, :, wide]
        dst_up, dst_down = X.at[below(s), 0, 0, :, wide], X.at[min(above(s), NZ - 1), 0, 0, :, wide]
        if s == FAR:
            src_up, dst_up = src_up.at[upper], dst_up.at[upper]
            src_down, dst_down = src_down.at[lower], dst_down.at[lower]
        send(src_up, dst_up, zr.at[s - 1], at_z(hop))
        send(src_down, dst_down, zr.at[s - 1], at_z(NZ - hop))

    def blocks(n):
        return X.at[pl.ds(0, n), 0, 0, :, wide]

    def strips(a, b):
        return X.at[0, pl.ds(0, a), pl.ds(0, b), :, narrow]

    def z_wait(s):
        arrived(blocks(2 if s < FAR else 1), zr.at[s - 1])

    def o_send(s):
        first, n = pair(s)
        at = pl.ds(first, n)
        if s == 0:
            def src(r):
                return hidden.at[r, wide]

            def dst(a, b, r):
                return X.at[0, a, b, r, wide]
        else:
            def src(r):
                return X.at[at, 0, 0, r, wide]

            def dst(a, b, r):
                return X.at[at, a, b, r, wide]
        plan = [((1, 0), both), ((0, 1), both), ((3, 0), both), ((0, 3), both), ((2, 0), upper), ((0, 2), lower)]
        for (dx, dy), r in plan:
            send(src(r), dst(-dx % NX, -dy % NY, r), orr.at[s], at_xy(dx, dy))

    def o_wait(s):
        arrived(blocks(5 * pair(s)[1]), orr.at[s])

    def v_send(s):
        at, rest = pl.ds(*pair(s)), pl.ds(1, 3)
        for d in (1, 3):
            send(X.at[at, rest, 0, upper, wide], X.at[at, rest, -d % NY, upper, wide],
                 vr.at[s], at_xy(0, d))
            send(X.at[at, 0, rest, lower, wide], X.at[at, -d % NX, rest, lower, wide],
                 vr.at[s], at_xy(d, 0))

    def v_wait(s):
        arrived(blocks(6 * pair(s)[1]), vr.at[s])

    def f_send(s):
        at = pl.ds(*pair(s))
        for i, d in enumerate((1, 3)):
            h = pl.ds(2 * i, 2)
            send(X.at[at, h, -d % NY, upper, wide], X.at[at, h, 2, upper, wide],
                 fr.at[s], at_xy(0, d))
            send(X.at[at, -d % NX, h, lower, wide], X.at[at, 2, h, lower, wide],
                 fr.at[s], at_xy(d, 0))

    def f_wait(s):
        arrived(blocks(4 * pair(s)[1]), fr.at[s])

    def a1_send():
        for d in (1, 3, 2):
            send(hidden.at[:, narrow], X.at[0, -d % NX, 0, :, narrow], ar.at[1], at_xy(d, 0))

    def a0_send():
        for d in (1, 3, 2):
            send(hidden.at[:, narrow], X.at[0, 0, -d % NY, :, narrow], ar.at[0], at_xy(0, d))

    def a0_wait():
        arrived(strips(1, 3), ar.at[0])

    def a2_send():
        arrived(strips(1, 3), ar.at[1])
        rest = pl.ds(1, 3)
        for d in (1, 3, 2):
            send(X.at[0, rest, 0, :, narrow], X.at[0, rest, -d % NY, :, narrow], ar.at[2], at_xy(0, d))

    def a2_wait():
        arrived(strips(3, 3), ar.at[2])

    def slab(j, h):
        if PIECES == NX:
            return X.at[j, pl.ds(h, 1), :, :, narrow]
        return X.at[j, pl.ds(h // 2, 1), pl.ds(2 * (h % 2), 2), :, narrow]

    def ring_send(s, h):
        if s < FAR or h < PIECES // 2:
            send(slab(below(s - 1), h), slab(below(s), h), rr.at[s - 1, h], at_z(1))
        if s < FAR or h >= PIECES // 2:
            send(slab(above(s - 1), h), slab(min(above(s), NZ - 1), h), rr.at[s - 1, h], at_z(NZ - 1))

    def ring_wait(s, h):
        n = NX * NY // PIECES * (2 if s < FAR else 1)
        arrived(strips(n // min(n, NY), min(n, NY)), rr.at[s - 1, h])

    def multiply(s):
        first, n = pair(s)
        if s == 0:
            arrived(W.at[:, pl.ds(0, SLOTS), :], wl)
            arrived(W.at[:, pl.ds(SLOTS, SLOTS), :], wr)

        @pl.loop(first, first + n)
        def _(j):
            part_sum = lax.dot_general(
                W[j], X[j].reshape(NX * NY * ROWS, WIDTH),
                (((1,), (1,)), ((), ())), preferred_element_type=jnp.float32)
            if s == 0:
                acc[...] = part_sum
            else:
                acc[...] += part_sum

    def all_left():
        assert sum(sent) == math.prod(X.shape) - ROWS * WIDTH
        arrived(X, out_sem)
        arrived(W.at[:, pl.ds(SLOTS, SLOTS), :], ws)

    for t in range(1, FAR + 1):
        if t == HOP[t - 1]:
            z_send(t)
    o_send(0)
    a1_send()
    a0_send()

    @pl.loop(0, NZ)
    def _(j):
        other_weight(j).start()
        own_weight(j).start()

    goals = [pltpu.make_async_copy(targets.at[(x + d) % NX], goal.at[d], gl.at[0]) for d in range(NX)]
    share_copy = pltpu.make_async_copy(shares, own_sh, gl.at[1])
    for g in goals + [share_copy]:
        g.start()
    pltpu.make_async_copy(hidden, spare, out_sem).start()

    def event(kind, s=0, h=0):
        if kind == "z":
            z_wait(s)
            for t in range(s + 1, FAR + 1):
                if t - HOP[t - 1] == s:
                    z_send(t)
            o_send(s)
        elif kind == "o":
            o_wait(s)
            v_send(s)
        elif kind == "v":
            v_wait(s)
            f_send(s)
        elif kind == "m":
            f_wait(s)
            multiply(s)
        elif kind == "a0":
            a0_wait()
            for h in range(PIECES // NX):
                ring_send(1, h)
        elif kind == "a2":
            a2_send()
        elif kind == "a3":
            a2_wait()
            for h in range(PIECES // NX, PIECES):
                ring_send(1, h)
        else:
            ring_wait(s, h)
            if s < FAR:
                ring_send(s + 1, h)

    own_block.wait()
    for name in ORDER:
        event(*name)

    def row_send(src, dst, send_sem, recv_sem, device):
        pltpu.make_async_remote_copy(
            src_ref=src, dst_ref=dst, send_sem=send_sem, recv_sem=recv_sem,
            device_id=device, device_id_type=MESH).start()

    def swap(dx):
        cols = pl.ds(dx * LANES, LANES)
        return pltpu.make_async_remote_copy(
            src_ref=acc.at[pl.ds(SLOTS, SLOTS), cols], dst_ref=part.at[:, cols],
            send_sem=ps, recv_sem=pr.at[dx], device_id=sibling, device_id_type=MESH)

    for dx in DXS:
        swap(dx).start()
    arrived(goal, gl.at[0])
    share_copy.wait()
    own_share = jnp.int32(0)
    offset = jnp.int32(0)
    for s in range(NX * NY):
        own_share = own_share + jnp.where(s == pipe, own_sh[s], 0)
        offset = offset + jnp.where(s < pipe, own_sh[s], 0)
    position = lax.broadcasted_iota(jnp.int32, (SLOTS, 1), 0) * (2 * NZ) + tensor
    live = position < own_share
    word = position + offset
    lane = lax.broadcasted_iota(jnp.int32, (1, LANES), 1)

    def packed(values, dy):
        top, total, pick = values
        moved = [pltpu.roll(v, (ROWS * (i - dy)) % LANES, 1) if (ROWS * (i - dy)) % LANES else v
                 for i, v in enumerate((top, total, pick))]
        return jnp.where(lane < ROWS, moved[0], jnp.where(lane < 2 * ROWS, moved[1], moved[2]))

    for dx in DXS:
        cols = pl.ds(dx * LANES, LANES)
        swap(dx).wait_recv()
        logits = acc[pl.ds(0, SLOTS), cols] + part[:, cols]
        want = goal[dx]
        turned = want
        for k in range(1, NY):
            turned = jnp.where(y == k, pltpu.roll(want, LANES - ROWS * k, 1), turned)
        top = jnp.max(jnp.where(live, logits, VERY_NEGATIVE), axis=0, keepdims=True)
        total = jnp.sum(jnp.where(live, jnp.exp(logits - top), 0.0), axis=0, keepdims=True)
        pick = jnp.sum(jnp.where(live & (word == turned), logits, 0.0), axis=0, keepdims=True)
        for dy in DXS:
            row = packed((top, total, pick), dy)
            if dx == 0 and dy == 0:
                sxy[0] = row
            else:
                pack[dx * NY + dy] = row
                to = (-dx % NX) * NY + (-dy % NY)
                row_send(pack.at[dx * NY + dy], sxy.at[to], xs, xr, at_xy(dx, dy))
    arrived(sxy.at[pl.ds(1, NX * NY - 1)], xr)
    sz[z] = join(sxy[...])
    for d in (8, 7, 9, 6, 10, 5, 11, 4, 12, 3, 13, 2, 14, 1, 15):
        row_send(sz.at[z], sz.at[z], ts, tr, at_z(d))
    arrived(part, ps)
    all_left()
    arrived(sz.at[pl.ds(1, NZ - 1)], tr)
    sc[c] = join(sz[...])
    row_send(sc.at[c], sc.at[c], cs, cr, sibling)
    arrived(sc.at[1 - c], cr)
    row = join(sc[...])
    log_total = pltpu.roll(row, ROWS, 1) + jnp.log(jnp.where((lane >= ROWS) & (lane < 2 * ROWS), row, 1.0))
    out[...] = jnp.where(lane < ROWS, row, jnp.where(
        lane < 2 * ROWS, log_total, row - pltpu.roll(log_total, ROWS, 1)))
    arrived(sxy.at[pl.ds(1, NX * NY - 1)], xs)
    arrived(sz.at[pl.ds(1, NZ - 1)], ts)
    arrived(sc.at[0], cs)


def local(hidden, head_weight, shares, targets):
    dma = pltpu.SemaphoreType.DMA
    rows = NX * NY * ROWS
    n = FAR + 1
    line = lambda k: pltpu.VMEM((k, 1, LANES), jnp.float32)
    hbm = pl.BlockSpec(memory_space=pltpu.HBM)
    out = pl.pallas_call(
        kernel,
        out_shape=jax.ShapeDtypeStruct((1, LANES), jnp.float32),
        in_specs=[hbm] * 4,
        out_specs=pl.BlockSpec(memory_space=pltpu.VMEM),
        scratch_shapes=[
            pltpu.VMEM((NZ, NX, NY, ROWS, WIDTH), jnp.bfloat16),
            pltpu.VMEM((NZ, 2 * SLOTS, WIDTH), jnp.bfloat16),
            pltpu.VMEM((2 * SLOTS, rows), jnp.float32),
            pltpu.VMEM((SLOTS, rows), jnp.float32),
            pltpu.VMEM((ROWS, WIDTH), jnp.bfloat16),
            pltpu.VMEM((NX, 1, LANES), jnp.int32),
            pltpu.SMEM((NX * NY,), jnp.int32),
            line(16), line(16), line(NZ), line(2),
            dma(()), dma((FAR,)), dma((3,)), dma((FAR, PIECES)), dma((n,)), dma((n,)), dma((n,)),
            dma(()), dma(()), dma(()), dma(()), dma((2,)), dma(()), dma((NX,)),
            *[dma(()) for _ in range(6)],
        ],
        compiler_params=pltpu.CompilerParams(
            collective_id=0, has_side_effects=True, vmem_limit_bytes=60 * 1024 * 1024),
        cost_estimate=pl.CostEstimate(
            flops=2 * rows * SLOTS * 2 * NZ * WIDTH, bytes_accessed=22 * 1024 * 1024,
            transcendentals=rows * SLOTS),
    )(hidden, head_weight, shares, targets.reshape(NX, 1, LANES))
    return tuple(out[0, ROWS * i:ROWS * (i + 1)] for i in range(3))


def solution(mesh):
    in_specs = (P("pipe", "tensor"), P(("pipe", "tensor"), None), P(), P())
    out_specs = (P("pipe"), P("pipe"), P("pipe"))
    return jax.shard_map(local, mesh=mesh, in_specs=in_specs, out_specs=out_specs, check_vma=False)
```

```python
import math

import jax
import jax.numpy as jnp
from jax import lax
from jax.experimental import pallas as pl
from jax.experimental.pallas import tpu as pltpu
from jax.sharding import PartitionSpec as P

VERY_NEGATIVE = -1e30
NX, NY, NZ = 4, 4, 16
FAR = NZ // 2
ROWS = 32
HALF = 16
WIDTH = 512
WIDE = 384
SLOTS = 144
LANES = 128
MESH = pl.DeviceIdType.MESH
HOP = (1,) * 8
PIECES = 8
ORDER = (
    ("z", 1), ("a0",), ("a2",), ("o", 0), ("z", 2), ("r", 1, 0), ("r", 1, 1), ("o", 1), ("v", 0), ("a3",),
    ("z", 3), ("r", 2, 0), ("r", 2, 1), ("o", 2), ("v", 1), ("m", 0), ("r", 1, 7), ("r", 1, 6), ("r", 1, 2),
    ("r", 1, 4), ("r", 1, 3), ("r", 1, 5), ("o", 3), ("r", 3, 0), ("r", 3, 1), ("z", 4), ("v", 2), ("r", 2,
    7), ("r", 2, 6), ("r", 2, 2), ("r", 2, 4), ("r", 2, 3), ("r", 2, 5), ("r", 4, 0), ("r", 4, 1), ("m", 1),
    ("z", 5), ("r", 3, 7), ("r", 3, 6), ("r", 3, 2), ("v", 3), ("r", 3, 4), ("r", 3, 3), ("o", 4), ("r", 3,
    5), ("r", 5, 0), ("r", 5, 1), ("z", 6), ("r", 4, 7), ("r", 4, 6), ("r", 4, 2), ("o", 5), ("r", 4, 4),
    ("r", 4, 3), ("r", 4, 5), ("r", 6, 0), ("r", 6, 1), ("m", 2), ("z", 7), ("r", 5, 7), ("r", 5, 6), ("v",
    4), ("r", 5, 2), ("r", 5, 4), ("r", 5, 3), ("o", 6), ("r", 5, 5), ("r", 7, 0), ("r", 7, 1), ("v", 5),
    ("z", 8), ("r", 6, 7), ("r", 6, 6), ("r", 6, 2), ("o", 7), ("r", 6, 4), ("r", 6, 3), ("r", 6, 5), ("r", 8,
    0), ("r", 8, 1), ("m", 3), ("r", 7, 7), ("r", 7, 6), ("v", 6), ("r", 7, 2), ("o", 8), ("r", 7, 4), ("r",
    7, 3), ("r", 7, 5), ("v", 7), ("m", 4), ("r", 8, 7), ("r", 8, 6), ("r", 8, 2), ("r", 8, 4), ("r", 8, 3),
    ("v", 8), ("r", 8, 5), ("m", 5), ("m", 6), ("m", 7), ("m", 8),
)
DXS = (2, 3, 1, 0)
LAST = (8,)


def below(s):
    return 2 * s - 1 if s else 0


def above(s):
    return 2 * s


def pair(s):
    if s == 0:
        return 0, 1
    return (2 * s - 1, 2) if s < FAR else (2 * FAR - 1, 1)


def join(v):
    lane = lax.broadcasted_iota(jnp.int32, (1, LANES), 1)
    middle = (lane >= ROWS) & (lane < 2 * ROWS)
    rows = [v[i] for i in range(v.shape[0])]
    top = rows[0]
    for r in rows[1:]:
        top = jnp.maximum(top, r)
    total = jnp.zeros_like(top)
    for r in rows:
        scale = pltpu.roll(jnp.exp(r - top), ROWS, 1)
        total = total + r * jnp.where(middle, scale, 1.0)
    return jnp.where(lane < ROWS, top, total)


def kernel(hidden, weight, shares, targets, out,
           X, W, acc, part, spare, goal, own_sh, pack, sxy, sz,
           out_sem, zr, ar, rr, orr, vr, fr, ws, wr, wl, hl, gl, ps, pr,
           xs, xr, ts, tr):
    pipe = lax.axis_index("pipe")
    tensor = lax.axis_index("tensor")
    x, y = pipe // NY, pipe % NY
    z, c = tensor // 2, tensor % 2

    def at_xy(dx, dy):
        return (((x + dx) % NX) * NY + (y + dy) % NY, tensor)

    def at_z(d):
        return (pipe, ((z + d) % NZ) * 2 + c)

    sibling = (pipe, z * 2 + 1 - c)
    sent = []

    def send(src, dst, recv_sem, device):
        pltpu.make_async_remote_copy(
            src_ref=src, dst_ref=dst, send_sem=out_sem, recv_sem=recv_sem,
            device_id=device, device_id_type=MESH).start()
        sent.append(math.prod(src.shape))

    def arrived(ref, sem):
        pltpu.make_async_copy(ref, ref, sem).wait()

    def feature_block(j, core):
        step = (j + 1) // 2
        at = jnp.where(j % 2 == 1, z + NZ - step, z + step) % NZ
        return pl.ds(pl.multiple_of((2 * at + core) * WIDTH, WIDTH), WIDTH)

    def own_weight(j):
        return pltpu.make_async_copy(
            weight.at[:, feature_block(j, c)], W.at[j, pl.ds(0, SLOTS), :], wl)

    def other_weight(j):
        return pltpu.make_async_remote_copy(
            src_ref=weight.at[:, feature_block(j, 1 - c)],
            dst_ref=W.at[j, pl.ds(SLOTS, SLOTS), :],
            send_sem=ws, recv_sem=wr, device_id=sibling, device_id_type=MESH)

    barrier = pltpu.get_barrier_semaphore()
    greet = [at_xy(1, 0), at_xy(3, 0), at_xy(0, 1), at_xy(0, 3), at_z(1), at_z(15),
             at_xy(2, 0), at_xy(0, 2), sibling]
    for device in greet:
        pl.semaphore_signal(barrier, inc=1, device_id=device, device_id_type=MESH)
    own_block = pltpu.make_async_copy(hidden, X.at[0, 0, 0], hl)
    own_block.start()
    pl.semaphore_wait(barrier, len(greet))

    wide, narrow = pl.ds(0, WIDE), pl.ds(WIDE, WIDTH - WIDE)
    upper, lower = pl.ds(0, HALF), pl.ds(HALF, HALF)
    both = pl.ds(0, ROWS)

    def z_send(s):
        hop = HOP[s - 1]
        if s == hop:
            src_up = src_down = hidden.at[:, wide]
        else:
            src_up, src_down = X.at[below(s - hop), 0, 0, :, wide], X.at[above(s - hop), 0, 0, :, wide]
        dst_up, dst_down = X.at[below(s), 0, 0, :, wide], X.at[min(above(s), NZ - 1), 0, 0, :, wide]
        if s == FAR:
            src_up, dst_up = src_up.at[upper], dst_up.at[upper]
            src_down, dst_down = src_down.at[lower], dst_down.at[lower]
        send(src_up, dst_up, zr.at[s - 1], at_z(hop))
        send(src_down, dst_down, zr.at[s - 1], at_z(NZ - hop))

    def blocks(n):
        return X.at[pl.ds(0, n), 0, 0, :, wide]

    def strips(a, b):
        return X.at[0, pl.ds(0, a), pl.ds(0, b), :, narrow]

    def z_wait(s):
        arrived(blocks(2 if s < FAR else 1), zr.at[s - 1])

    def o_send(s):
        first, n = pair(s)
        at = pl.ds(first, n)
        if s == 0:
            def src(r):
                return hidden.at[r, wide]

            def dst(a, b, r):
                return X.at[0, a, b, r, wide]
        else:
            def src(r):
                return X.at[at, 0, 0, r, wide]

            def dst(a, b, r):
                return X.at[at, a, b, r, wide]
        plan = [((1, 0), both), ((0, 1), both), ((3, 0), both), ((0, 3), both), ((2, 0), upper), ((0, 2), lower)]
        for (dx, dy), r in plan:
            send(src(r), dst(-dx % NX, -dy % NY, r), orr.at[s], at_xy(dx, dy))

    def o_wait(s):
        arrived(blocks(5 * pair(s)[1]), orr.at[s])

    def v_send(s):
        at, rest = pl.ds(*pair(s)), pl.ds(1, 3)
        for d in (1, 3):
            send(X.at[at, rest, 0, upper, wide], X.at[at, rest, -d % NY, upper, wide],
                 vr.at[s], at_xy(0, d))
            send(X.at[at, 0, rest, lower, wide], X.at[at, -d % NX, rest, lower, wide],
                 vr.at[s], at_xy(d, 0))

    def v_wait(s):
        arrived(blocks(6 * pair(s)[1]), vr.at[s])

    def f_send(s):
        at = pl.ds(*pair(s))
        for i, d in enumerate((1, 3)):
            h = pl.ds(2 * i, 2)
            send(X.at[at, h, -d % NY, upper, wide], X.at[at, h, 2, upper, wide],
                 fr.at[s], at_xy(0, d))
            send(X.at[at, -d % NX, h, lower, wide], X.at[at, 2, h, lower, wide],
                 fr.at[s], at_xy(d, 0))

    def f_wait(s):
        arrived(blocks(4 * pair(s)[1]), fr.at[s])

    def a1_send():
        for d in (1, 3, 2):
            send(hidden.at[:, narrow], X.at[0, -d % NX, 0, :, narrow], ar.at[1], at_xy(d, 0))

    def a0_send():
        for d in (1, 3, 2):
            send(hidden.at[:, narrow], X.at[0, 0, -d % NY, :, narrow], ar.at[0], at_xy(0, d))

    def a0_wait():
        arrived(strips(1, 3), ar.at[0])

    def a2_send():
        arrived(strips(1, 3), ar.at[1])
        rest = pl.ds(1, 3)
        for d in (1, 3, 2):
            send(X.at[0, rest, 0, :, narrow], X.at[0, rest, -d % NY, :, narrow], ar.at[2], at_xy(0, d))

    def a2_wait():
        arrived(strips(3, 3), ar.at[2])

    def slab(j, h):
        if PIECES == NX:
            return X.at[j, pl.ds(h, 1), :, :, narrow]
        return X.at[j, pl.ds(h // 2, 1), pl.ds(2 * (h % 2), 2), :, narrow]

    def ring_send(s, h):
        if s < FAR or h < PIECES // 2:
            send(slab(below(s - 1), h), slab(below(s), h), rr.at[s - 1, h], at_z(1))
        if s < FAR or h >= PIECES // 2:
            send(slab(above(s - 1), h), slab(min(above(s), NZ - 1), h), rr.at[s - 1, h], at_z(NZ - 1))

    def ring_wait(s, h):
        n = NX * NY // PIECES * (2 if s < FAR else 1)
        arrived(strips(n // min(n, NY), min(n, NY)), rr.at[s - 1, h])

    def row_send(src, dst, send_sem, recv_sem, device):
        pltpu.make_async_remote_copy(
            src_ref=src, dst_ref=dst, send_sem=send_sem, recv_sem=recv_sem,
            device_id=device, device_id_type=MESH).start()

    def swap(dx):
        cols = pl.ds(dx * LANES, LANES)
        return pltpu.make_async_remote_copy(
            src_ref=acc.at[pl.ds(SLOTS, SLOTS), cols], dst_ref=part.at[:, cols],
            send_sem=ps, recv_sem=pr.at[dx], device_id=sibling, device_id_type=MESH)

    def multiply_last():
        first, n = pair(LAST[0])[0], sum(pair(s)[1] for s in LAST)

        def add(slots, x0):
            cols = pl.ds(x0 * LANES, 2 * LANES)
            total = acc[slots, cols]
            for j in range(first, first + n):
                total += lax.dot_general(
                    W[j, slots, :], X[j, pl.ds(x0, 2)].reshape(2 * NY * ROWS, WIDTH),
                    (((1,), (1,)), ((), ())), preferred_element_type=jnp.float32)
            acc[slots, cols] = total

        for x0 in (2, 0):
            add(pl.ds(SLOTS, SLOTS), x0)
            for dx in DXS:
                if dx // 2 == x0 // 2:
                    swap(dx).start()
        for x0 in (2, 0):
            add(pl.ds(0, SLOTS), x0)

    def multiply(s):
        first, n = pair(s)
        if s == 0:
            arrived(W.at[:, pl.ds(0, SLOTS), :], wl)
            arrived(W.at[:, pl.ds(SLOTS, SLOTS), :], wr)

        @pl.loop(first, first + n)
        def _(j):
            part_sum = lax.dot_general(
                W[j], X[j].reshape(NX * NY * ROWS, WIDTH),
                (((1,), (1,)), ((), ())), preferred_element_type=jnp.float32)
            if s == 0:
                acc[...] = part_sum
            else:
                acc[...] += part_sum

    def all_left():
        assert sum(sent) == math.prod(X.shape) - ROWS * WIDTH
        arrived(X, out_sem)
        arrived(W.at[:, pl.ds(SLOTS, SLOTS), :], ws)

    for t in range(1, FAR + 1):
        if t == HOP[t - 1]:
            z_send(t)
    o_send(0)
    a1_send()
    a0_send()

    @pl.loop(0, NZ)
    def _(j):
        other_weight(j).start()
        own_weight(j).start()

    goals = [pltpu.make_async_copy(targets.at[(x + d) % NX], goal.at[d], gl.at[0]) for d in range(NX)]
    share_copy = pltpu.make_async_copy(shares, own_sh, gl.at[1])
    for g in goals + [share_copy]:
        g.start()
    pltpu.make_async_copy(hidden, spare, out_sem).start()

    known = {}

    def prepare():
        arrived(goal, gl.at[0])
        share_copy.wait()
        own_share = jnp.int32(0)
        offset = jnp.int32(0)
        for s in range(NX * NY):
            own_share = own_share + jnp.where(s == pipe, own_sh[s], 0)
            offset = offset + jnp.where(s < pipe, own_sh[s], 0)
        known["share"] = own_share
        for dx in range(NX):
            want = goal[dx] - offset
            turned = want
            for k in range(1, NY):
                turned = jnp.where(y == k, pltpu.roll(want, LANES - ROWS * k, 1), turned)
            goal[dx] = turned

    def event(kind, s=0, h=0):
        if kind == "z":
            z_wait(s)
            for t in range(s + 1, FAR + 1):
                if t - HOP[t - 1] == s:
                    z_send(t)
            o_send(s)
        elif kind == "o":
            o_wait(s)
            v_send(s)
        elif kind == "v":
            v_wait(s)
            f_send(s)
        elif kind == "m":
            f_wait(s)
            if s not in LAST:
                multiply(s)
        elif kind == "a0":
            a0_wait()
            for h in range(PIECES // NX):
                ring_send(1, h)
        elif kind == "a2":
            a2_send()
        elif kind == "a3":
            a2_wait()
            for h in range(PIECES // NX, PIECES):
                ring_send(1, h)
        else:
            ring_wait(s, h)
            if s < FAR:
                ring_send(s + 1, h)

    own_block.wait()
    for name in ORDER:
        event(*name)
        if name == ("m", 0):
            prepare()
    multiply_last()

    lane = lax.broadcasted_iota(jnp.int32, (1, LANES), 1)

    def packed(values, dy):
        top, total, pick = values
        moved = [pltpu.roll(v, (ROWS * (i - dy)) % LANES, 1) if (ROWS * (i - dy)) % LANES else v
                 for i, v in enumerate((top, total, pick))]
        return jnp.where(lane < ROWS, moved[0], jnp.where(lane < 2 * ROWS, moved[1], moved[2]))

    position = lax.broadcasted_iota(jnp.int32, (SLOTS, LANES), 0) * (2 * NZ) + tensor
    live = position < known["share"]
    for dx in DXS:
        cols = pl.ds(dx * LANES, LANES)
        swap(dx).wait_recv()
        logits = acc[pl.ds(0, SLOTS), cols] + part[:, cols]
        top = jnp.max(jnp.where(live, logits, VERY_NEGATIVE), axis=0, keepdims=True)
        total = jnp.sum(jnp.where(live, jnp.exp(logits - top), 0.0), axis=0, keepdims=True)
        pick = jnp.sum(jnp.where(live & (position == goal[dx]), logits, 0.0), axis=0, keepdims=True)
        for dy in DXS:
            row = packed((top, total, pick), dy)
            to = c * NX * NY + (-dx % NX) * NY + (-dy % NY)
            if dx == 0 and dy == 0:
                sxy[to] = row
                row_send(sxy.at[to], sxy.at[to], xs, xr, sibling)
            else:
                pack[dx * NY + dy] = row
                for core in range(2):
                    device = (at_xy(dx, dy)[0], z * 2 + core)
                    row_send(pack.at[dx * NY + dy], sxy.at[to], xs, xr, device)
    arrived(sxy.at[pl.ds(1, 2 * NX * NY - 1)], xr)
    sz[z] = join(sxy[...])
    for d in (8, 7, 9, 6, 10, 5, 11, 4, 12, 3, 13, 2, 14, 1, 15):
        row_send(sz.at[z], sz.at[z], ts, tr, at_z(d))
    arrived(part, ps)
    all_left()
    arrived(sz.at[pl.ds(1, NZ - 1)], tr)
    row = join(sz[...])
    log_total = pltpu.roll(row, ROWS, 1) + jnp.log(jnp.where((lane >= ROWS) & (lane < 2 * ROWS), row, 1.0))
    out[...] = jnp.where(lane < ROWS, row, jnp.where(
        lane < 2 * ROWS, log_total, row - pltpu.roll(log_total, ROWS, 1)))
    arrived(sxy.at[pl.ds(1, 2 * NX * NY - 1)], xs)
    arrived(sz.at[pl.ds(1, NZ - 1)], ts)


def local(hidden, head_weight, shares, targets):
    dma = pltpu.SemaphoreType.DMA
    rows = NX * NY * ROWS
    n = FAR + 1
    line = lambda k: pltpu.VMEM((k, 1, LANES), jnp.float32)
    hbm = pl.BlockSpec(memory_space=pltpu.HBM)
    out = pl.pallas_call(
        kernel,
        out_shape=jax.ShapeDtypeStruct((1, LANES), jnp.float32),
        in_specs=[hbm] * 4,
        out_specs=pl.BlockSpec(memory_space=pltpu.VMEM),
        scratch_shapes=[
            pltpu.VMEM((NZ, NX, NY, ROWS, WIDTH), jnp.bfloat16),
            pltpu.VMEM((NZ, 2 * SLOTS, WIDTH), jnp.bfloat16),
            pltpu.VMEM((2 * SLOTS, rows), jnp.float32),
            pltpu.VMEM((SLOTS, rows), jnp.float32),
            pltpu.VMEM((ROWS, WIDTH), jnp.bfloat16),
            pltpu.VMEM((NX, 1, LANES), jnp.int32),
            pltpu.SMEM((NX * NY,), jnp.int32),
            line(NX * NY), line(2 * NX * NY), line(NZ),
            dma(()), dma((FAR,)), dma((3,)), dma((FAR, PIECES)), dma((n,)), dma((n,)), dma((n,)),
            dma(()), dma(()), dma(()), dma(()), dma((2,)), dma(()), dma((NX,)),
            *[dma(()) for _ in range(4)],
        ],
        compiler_params=pltpu.CompilerParams(
            collective_id=0, has_side_effects=True, vmem_limit_bytes=60 * 1024 * 1024),
        cost_estimate=pl.CostEstimate(
            flops=2 * rows * SLOTS * 2 * NZ * WIDTH, bytes_accessed=22 * 1024 * 1024,
            transcendentals=rows * SLOTS),
    )(hidden, head_weight, shares, targets.reshape(NX, 1, LANES))
    return tuple(out[0, ROWS * i:ROWS * (i + 1)] for i in range(3))


def solution(mesh):
    in_specs = (P("pipe", "tensor"), P(("pipe", "tensor"), None), P(), P())
    out_specs = (P("pipe"), P("pipe"), P("pipe"))
    return jax.shard_map(local, mesh=mesh, in_specs=in_specs, out_specs=out_specs, check_vma=False)
```

```python
import math

import jax
import jax.numpy as jnp
from jax import lax
from jax.experimental import pallas as pl
from jax.experimental.pallas import tpu as pltpu
from jax.sharding import PartitionSpec as P

VERY_NEGATIVE = -1e30
NX, NY, NZ = 4, 4, 16
FAR = NZ // 2
ROWS = 32
HALF = 16
WIDTH = 512
WIDE = 384
SLOTS = 144
LANES = 128
MESH = pl.DeviceIdType.MESH
HOP = (1,) * 8
PIECES = 4
ORDER = (
    ("z", 1), ("a0",), ("a2",), ("o", 0), ("z", 2), ("r", 1, 0), ("o", 1), ("z", 3), ("v", 0), ("a3",), ("r",
    2, 0), ("o", 2), ("z", 4), ("v", 1), ("m", 0, 0), ("o", 3), ("r", 1, 3), ("r", 1, 2), ("r", 1, 1), ("r",
    3, 0), ("z", 5), ("v", 2), ("o", 4), ("m", 1, 0), ("r", 2, 3), ("m", 1, 1), ("r", 2, 2), ("z", 6), ("r",
    2, 1), ("r", 4, 0), ("o", 5), ("v", 3), ("r", 3, 3), ("m", 2, 0), ("m", 2, 1), ("r", 3, 2), ("z", 7),
    ("v", 4), ("r", 3, 1), ("r", 5, 0), ("r", 4, 3), ("o", 6), ("m", 3, 0), ("z", 8), ("r", 4, 2), ("m", 3,
    1), ("v", 5), ("r", 4, 1), ("r", 6, 0), ("r", 5, 3), ("o", 7), ("m", 4, 0), ("r", 5, 2), ("m", 4, 1),
    ("o", 8), ("r", 5, 1), ("v", 6), ("m", 5, 0), ("r", 7, 0), ("r", 6, 3), ("m", 5, 1), ("r", 6, 2), ("v",
    7), ("v", 8), ("r", 6, 1), ("m", 6, 0), ("m", 6, 1), ("r", 8, 0), ("r", 7, 3), ("r", 7, 2), ("r", 7, 1),
    ("m", 7, 0), ("m", 7, 1), ("r", 8, 3), ("r", 8, 2), ("r", 8, 1), ("m", 8, 0),
)
DXS = (2, 3, 1, 0)
LAST = (8,)


def below(s):
    return 2 * s - 1 if s else 0


def above(s):
    return 2 * s


def pair(s):
    if s == 0:
        return 0, 1
    return (2 * s - 1, 2) if s < FAR else (2 * FAR - 1, 1)


def join(v):
    lane = lax.broadcasted_iota(jnp.int32, (1, LANES), 1)
    middle = (lane >= ROWS) & (lane < 2 * ROWS)
    rows = [v[i] for i in range(v.shape[0])]
    top = rows[0]
    for r in rows[1:]:
        top = jnp.maximum(top, r)
    total = jnp.zeros_like(top)
    for r in rows:
        scale = pltpu.roll(jnp.exp(r - top), ROWS, 1)
        total = total + r * jnp.where(middle, scale, 1.0)
    return jnp.where(lane < ROWS, top, total)


def kernel(hidden, weight, shares, targets, out,
           X, W, acc, part, spare, goal, own_sh, pack, sxy, sz,
           out_sem, zr, ar, rr, orr, vr, fr, ws, wr, wl, hl, gl, ps, pr,
           xs, xr, ts, tr):
    pipe = lax.axis_index("pipe")
    tensor = lax.axis_index("tensor")
    x, y = pipe // NY, pipe % NY
    z, c = tensor // 2, tensor % 2

    def at_xy(dx, dy):
        return (((x + dx) % NX) * NY + (y + dy) % NY, tensor)

    def at_z(d):
        return (pipe, ((z + d) % NZ) * 2 + c)

    sibling = (pipe, z * 2 + 1 - c)
    sent = []

    def send(src, dst, recv_sem, device):
        pltpu.make_async_remote_copy(
            src_ref=src, dst_ref=dst, send_sem=out_sem, recv_sem=recv_sem,
            device_id=device, device_id_type=MESH).start()
        sent.append(math.prod(src.shape))

    def arrived(ref, sem):
        pltpu.make_async_copy(ref, ref, sem).wait()

    def feature_block(j, core):
        step = (j + 1) // 2
        at = jnp.where(j % 2 == 1, z + NZ - step, z + step) % NZ
        return pl.ds(pl.multiple_of((2 * at + core) * WIDTH, WIDTH), WIDTH)

    def own_weight(j):
        return pltpu.make_async_copy(
            weight.at[:, feature_block(j, c)], W.at[j, pl.ds(0, SLOTS), :], wl)

    def other_weight(j):
        return pltpu.make_async_remote_copy(
            src_ref=weight.at[:, feature_block(j, 1 - c)],
            dst_ref=W.at[j, pl.ds(SLOTS, SLOTS), :],
            send_sem=ws, recv_sem=wr, device_id=sibling, device_id_type=MESH)

    barrier = pltpu.get_barrier_semaphore()
    greet = [at_xy(1, 0), at_xy(3, 0), at_xy(0, 1), at_xy(0, 3), at_z(1), at_z(15),
             at_xy(2, 0), at_xy(0, 2), sibling]
    for device in greet:
        pl.semaphore_signal(barrier, inc=1, device_id=device, device_id_type=MESH)
    own_block = pltpu.make_async_copy(hidden, X.at[0, 0, 0], hl)
    own_block.start()
    pl.semaphore_wait(barrier, len(greet))

    wide, narrow = pl.ds(0, WIDE), pl.ds(WIDE, WIDTH - WIDE)
    upper, lower = pl.ds(0, HALF), pl.ds(HALF, HALF)
    both = pl.ds(0, ROWS)

    def z_send(s):
        hop = HOP[s - 1]
        if s == hop:
            src_up = src_down = hidden.at[:, wide]
        else:
            src_up, src_down = X.at[below(s - hop), 0, 0, :, wide], X.at[above(s - hop), 0, 0, :, wide]
        dst_up, dst_down = X.at[below(s), 0, 0, :, wide], X.at[min(above(s), NZ - 1), 0, 0, :, wide]
        if s == FAR:
            src_up, dst_up = src_up.at[upper], dst_up.at[upper]
            src_down, dst_down = src_down.at[lower], dst_down.at[lower]
        send(src_up, dst_up, zr.at[s - 1], at_z(hop))
        send(src_down, dst_down, zr.at[s - 1], at_z(NZ - hop))

    def blocks(n):
        return X.at[pl.ds(0, n), 0, 0, :, wide]

    def strips(a, b):
        return X.at[0, pl.ds(0, a), pl.ds(0, b), :, narrow]

    def z_wait(s):
        arrived(blocks(2 if s < FAR else 1), zr.at[s - 1])

    def o_send(s):
        first, n = pair(s)
        at = pl.ds(first, n)
        if s == 0:
            def src(r):
                return hidden.at[r, wide]

            def dst(a, b, r):
                return X.at[0, a, b, r, wide]
        else:
            def src(r):
                return X.at[at, 0, 0, r, wide]

            def dst(a, b, r):
                return X.at[at, a, b, r, wide]
        plan = [((1, 0), both), ((0, 1), both), ((3, 0), both), ((0, 3), both), ((2, 0), upper), ((0, 2), lower)]
        for (dx, dy), r in plan:
            send(src(r), dst(-dx % NX, -dy % NY, r), orr.at[s], at_xy(dx, dy))

    def o_wait(s):
        arrived(blocks(5 * pair(s)[1]), orr.at[s])

    def v_send(s):
        at, rest = pl.ds(*pair(s)), pl.ds(1, 3)
        for d in (1, 3):
            send(X.at[at, rest, 0, upper, wide], X.at[at, rest, -d % NY, upper, wide],
                 vr.at[s], at_xy(0, d))
            send(X.at[at, 0, rest, lower, wide], X.at[at, -d % NX, rest, lower, wide],
                 vr.at[s], at_xy(d, 0))

    def v_wait(s):
        arrived(blocks(6 * pair(s)[1]), vr.at[s])

    def f_send(s):
        at = pl.ds(*pair(s))
        for i, d in enumerate((1, 3)):
            h = pl.ds(2 * i, 2)
            send(X.at[at, h, -d % NY, upper, wide], X.at[at, h, 2, upper, wide],
                 fr.at[s], at_xy(0, d))
            send(X.at[at, -d % NX, h, lower, wide], X.at[at, 2, h, lower, wide],
                 fr.at[s], at_xy(d, 0))

    def f_wait(s):
        arrived(blocks(4 * pair(s)[1]), fr.at[s])

    def a1_send():
        for d in (1, 3, 2):
            send(hidden.at[:, narrow], X.at[0, -d % NX, 0, :, narrow], ar.at[1], at_xy(d, 0))

    def a0_send():
        for d in (1, 3, 2):
            send(hidden.at[:, narrow], X.at[0, 0, -d % NY, :, narrow], ar.at[0], at_xy(0, d))

    def a0_wait():
        arrived(strips(1, 3), ar.at[0])

    def a2_send():
        arrived(strips(1, 3), ar.at[1])
        rest = pl.ds(1, 3)
        for d in (1, 3, 2):
            send(X.at[0, rest, 0, :, narrow], X.at[0, rest, -d % NY, :, narrow], ar.at[2], at_xy(0, d))

    def a2_wait():
        arrived(strips(3, 3), ar.at[2])

    def slab(j, h):
        if PIECES == NX:
            return X.at[j, pl.ds(h, 1), :, :, narrow]
        return X.at[j, pl.ds(h // 2, 1), pl.ds(2 * (h % 2), 2), :, narrow]

    def ring_send(s, h):
        if s < FAR or h < PIECES // 2:
            send(slab(below(s - 1), h), slab(below(s), h), rr.at[s - 1, h], at_z(1))
        if s < FAR or h >= PIECES // 2:
            send(slab(above(s - 1), h), slab(min(above(s), NZ - 1), h), rr.at[s - 1, h], at_z(NZ - 1))

    def ring_wait(s, h):
        n = NX * NY // PIECES * (2 if s < FAR else 1)
        arrived(strips(n // min(n, NY), min(n, NY)), rr.at[s - 1, h])

    def row_send(src, dst, send_sem, recv_sem, device):
        pltpu.make_async_remote_copy(
            src_ref=src, dst_ref=dst, send_sem=send_sem, recv_sem=recv_sem,
            device_id=device, device_id_type=MESH).start()

    def swap(dx):
        cols = pl.ds(dx * LANES, LANES)
        return pltpu.make_async_remote_copy(
            src_ref=acc.at[pl.ds(SLOTS, SLOTS), cols], dst_ref=part.at[:, cols],
            send_sem=ps, recv_sem=pr.at[dx], device_id=sibling, device_id_type=MESH)

    def multiply_last():
        first, n = pair(LAST[0])[0], sum(pair(s)[1] for s in LAST)

        def add(slots, x0):
            cols = pl.ds(x0 * LANES, 2 * LANES)
            total = acc[slots, cols]
            for j in range(first, first + n):
                total += lax.dot_general(
                    W[j, slots, :], X[j, pl.ds(x0, 2)].reshape(2 * NY * ROWS, WIDTH),
                    (((1,), (1,)), ((), ())), preferred_element_type=jnp.float32)
            acc[slots, cols] = total

        for x0 in (2, 0):
            add(pl.ds(SLOTS, SLOTS), x0)
            for dx in DXS:
                if dx // 2 == x0 // 2:
                    swap(dx).start()
        for x0 in (2, 0):
            add(pl.ds(0, SLOTS), x0)

    def multiply(s, h):
        if s == 0:
            arrived(W.at[:, pl.ds(0, SLOTS), :], wl)
            arrived(W.at[:, pl.ds(SLOTS, SLOTS), :], wr)
        j = pair(s)[0] + h
        product = lax.dot_general(
            W[j], X[j].reshape(NX * NY * ROWS, WIDTH),
            (((1,), (1,)), ((), ())), preferred_element_type=jnp.float32)
        if s == 0:
            acc[...] = product
        else:
            acc[...] += product

    def all_left():
        assert sum(sent) == math.prod(X.shape) - ROWS * WIDTH
        arrived(X, out_sem)
        arrived(W.at[:, pl.ds(SLOTS, SLOTS), :], ws)

    for t in range(1, FAR + 1):
        if t == HOP[t - 1]:
            z_send(t)
    o_send(0)
    a1_send()
    a0_send()

    def weights():
        @pl.loop(0, NZ)
        def _(j):
            other_weight(j).start()
            own_weight(j).start()

    goals = [pltpu.make_async_copy(targets.at[(x + d) % NX], goal.at[d], gl.at[0]) for d in range(NX)]
    share_copy = pltpu.make_async_copy(shares, own_sh, gl.at[1])
    for g in goals + [share_copy]:
        g.start()
    pltpu.make_async_copy(hidden, spare, out_sem).start()

    known = {}

    def prepare():
        arrived(goal, gl.at[0])
        share_copy.wait()
        own_share = jnp.int32(0)
        offset = jnp.int32(0)
        for s in range(NX * NY):
            own_share = own_share + jnp.where(s == pipe, own_sh[s], 0)
            offset = offset + jnp.where(s < pipe, own_sh[s], 0)
        known["share"] = own_share
        for dx in range(NX):
            want = goal[dx] - offset
            turned = want
            for k in range(1, NY):
                turned = jnp.where(y == k, pltpu.roll(want, LANES - ROWS * k, 1), turned)
            goal[dx] = turned

    def event(kind, s=0, h=0):
        if kind == "z":
            z_wait(s)
            for t in range(s + 1, FAR + 1):
                if t - HOP[t - 1] == s:
                    z_send(t)
            o_send(s)
        elif kind == "o":
            o_wait(s)
            v_send(s)
        elif kind == "v":
            v_wait(s)
            f_send(s)
        elif kind == "m":
            if h == 0:
                f_wait(s)
            if s not in LAST:
                multiply(s, h)
        elif kind == "a0":
            a0_wait()
            for h in range(PIECES // NX):
                ring_send(1, h)
        elif kind == "a2":
            a2_send()
        elif kind == "a3":
            a2_wait()
            for h in range(PIECES // NX, PIECES):
                ring_send(1, h)
        else:
            ring_wait(s, h)
            if s < FAR:
                ring_send(s + 1, h)

    own_block.wait()
    for number, name in enumerate(ORDER, 1):
        event(*name)
        if number == 2:
            weights()
        if name == ("m", 0, 0):
            prepare()
    multiply_last()

    lane = lax.broadcasted_iota(jnp.int32, (1, LANES), 1)

    def packed(values, dy):
        top, total, pick = values
        moved = [pltpu.roll(v, (ROWS * (i - dy)) % LANES, 1) if (ROWS * (i - dy)) % LANES else v
                 for i, v in enumerate((top, total, pick))]
        return jnp.where(lane < ROWS, moved[0], jnp.where(lane < 2 * ROWS, moved[1], moved[2]))

    position = lax.broadcasted_iota(jnp.int32, (SLOTS, LANES), 0) * (2 * NZ) + tensor
    live = position < known["share"]
    for dx in DXS:
        cols = pl.ds(dx * LANES, LANES)
        swap(dx).wait_recv()
        logits = acc[pl.ds(0, SLOTS), cols] + part[:, cols]
        top = jnp.max(jnp.where(live, logits, VERY_NEGATIVE), axis=0, keepdims=True)
        total = jnp.sum(jnp.where(live, jnp.exp(logits - top), 0.0), axis=0, keepdims=True)
        pick = jnp.sum(jnp.where(live & (position == goal[dx]), logits, 0.0), axis=0, keepdims=True)
        for dy in DXS:
            row = packed((top, total, pick), dy)
            to = c * NX * NY + (-dx % NX) * NY + (-dy % NY)
            if dx == 0 and dy == 0:
                sxy[to] = row
                row_send(sxy.at[to], sxy.at[to], xs, xr, sibling)
            else:
                pack[dx * NY + dy] = row
                for core in range(2):
                    device = (at_xy(dx, dy)[0], z * 2 + core)
                    row_send(pack.at[dx * NY + dy], sxy.at[to], xs, xr, device)
    arrived(sxy.at[pl.ds(1, 2 * NX * NY - 1)], xr)
    sz[z] = join(sxy[...])
    for d in (8, 7, 9, 6, 10, 5, 11, 4, 12, 3, 13, 2, 14, 1, 15):
        row_send(sz.at[z], sz.at[z], ts, tr, at_z(d))
    arrived(part, ps)
    all_left()
    arrived(sz.at[pl.ds(1, NZ - 1)], tr)
    row = join(sz[...])
    log_total = pltpu.roll(row, ROWS, 1) + jnp.log(jnp.where((lane >= ROWS) & (lane < 2 * ROWS), row, 1.0))
    out[...] = jnp.where(lane < ROWS, row, jnp.where(
        lane < 2 * ROWS, log_total, row - pltpu.roll(log_total, ROWS, 1)))
    arrived(sxy.at[pl.ds(1, 2 * NX * NY - 1)], xs)
    arrived(sz.at[pl.ds(1, NZ - 1)], ts)


def local(hidden, head_weight, shares, targets):
    dma = pltpu.SemaphoreType.DMA
    rows = NX * NY * ROWS
    n = FAR + 1
    line = lambda k: pltpu.VMEM((k, 1, LANES), jnp.float32)
    hbm = pl.BlockSpec(memory_space=pltpu.HBM)
    out = pl.pallas_call(
        kernel,
        out_shape=jax.ShapeDtypeStruct((1, LANES), jnp.float32),
        in_specs=[hbm] * 4,
        out_specs=pl.BlockSpec(memory_space=pltpu.VMEM),
        scratch_shapes=[
            pltpu.VMEM((NZ, NX, NY, ROWS, WIDTH), jnp.bfloat16),
            pltpu.VMEM((NZ, 2 * SLOTS, WIDTH), jnp.bfloat16),
            pltpu.VMEM((2 * SLOTS, rows), jnp.float32),
            pltpu.VMEM((SLOTS, rows), jnp.float32),
            pltpu.VMEM((ROWS, WIDTH), jnp.bfloat16),
            pltpu.VMEM((NX, 1, LANES), jnp.int32),
            pltpu.SMEM((NX * NY,), jnp.int32),
            line(NX * NY), line(2 * NX * NY), line(NZ),
            dma(()), dma((FAR,)), dma((3,)), dma((FAR, PIECES)), dma((n,)), dma((n,)), dma((n,)),
            dma(()), dma(()), dma(()), dma(()), dma((2,)), dma(()), dma((NX,)),
            *[dma(()) for _ in range(4)],
        ],
        compiler_params=pltpu.CompilerParams(
            collective_id=0, has_side_effects=True, vmem_limit_bytes=60 * 1024 * 1024),
        cost_estimate=pl.CostEstimate(
            flops=2 * rows * SLOTS * 2 * NZ * WIDTH, bytes_accessed=22 * 1024 * 1024,
            transcendentals=rows * SLOTS),
    )(hidden, head_weight, shares, targets.reshape(NX, 1, LANES))
    return tuple(out[0, ROWS * i:ROWS * (i + 1)] for i in range(3))


def solution(mesh):
    in_specs = (P("pipe", "tensor"), P(("pipe", "tensor"), None), P(), P())
    out_specs = (P("pipe"), P("pipe"), P("pipe"))
    return jax.shard_map(local, mesh=mesh, in_specs=in_specs, out_specs=out_specs, check_vma=False)
```

```python
import math

import jax
import jax.numpy as jnp
from jax import lax
from jax.experimental import pallas as pl
from jax.experimental.pallas import tpu as pltpu
from jax.sharding import PartitionSpec as P

VERY_NEGATIVE = -1e30
NX, NY, NZ = 4, 4, 16
FAR = NZ // 2
ROWS = 32
HALF = 16
WIDTH = 512
WIDE = 384
SLOTS = 144
LANES = 128
MESH = pl.DeviceIdType.MESH
HOP = (1,) * 8
PIECES = 8
ORDER = (
    ("z", 1), ("a2",), ("a0",), ("o", 0), ("z", 2), ("r", 1, 1), ("r", 1, 0), ("o", 1), ("a3",), ("z", 3),
    ("v", 0), ("r", 2, 1), ("o", 2), ("r", 2, 0), ("r", 1, 6), ("r", 1, 5), ("r", 1, 7), ("r", 1, 3), ("r", 1,
    2), ("r", 1, 4), ("v", 1), ("r", 3, 1), ("z", 4), ("r", 3, 0), ("o", 3), ("v", 2), ("r", 2, 6), ("m", 0),
    ("r", 2, 5), ("r", 2, 7), ("r", 2, 3), ("r", 2, 2), ("r", 2, 4), ("r", 4, 1), ("r", 4, 0), ("z", 5), ("r",
    3, 6), ("m", 1), ("r", 3, 5), ("r", 3, 7), ("r", 3, 3), ("r", 3, 2), ("o", 4), ("r", 3, 4), ("r", 5, 1),
    ("r", 5, 0), ("z", 6), ("r", 4, 6), ("v", 3), ("m", 2), ("r", 4, 5), ("o", 5), ("r", 4, 7), ("r", 4, 3),
    ("r", 4, 2), ("r", 4, 4), ("r", 6, 1), ("r", 6, 0), ("r", 5, 6), ("z", 7), ("v", 4), ("r", 5, 5), ("r", 5,
    7), ("r", 5, 3), ("o", 6), ("r", 5, 2), ("m", 3), ("r", 5, 4), ("r", 7, 1), ("r", 7, 0), ("z", 8), ("r",
    6, 6), ("r", 6, 5), ("r", 6, 7), ("v", 5), ("r", 6, 3), ("r", 6, 2), ("o", 7), ("m", 4), ("r", 6, 4),
    ("r", 8, 1), ("r", 7, 6), ("v", 6), ("r", 7, 5), ("r", 7, 7), ("o", 8), ("r", 7, 3), ("r", 7, 2), ("r", 8,
    0), ("m", 5), ("r", 7, 4), ("v", 7), ("r", 8, 6), ("r", 8, 5), ("r", 8, 7), ("m", 6), ("v", 8), ("r", 8,
    3), ("r", 8, 2), ("r", 8, 4), ("m", 7), ("m", 8),
)
DXS = (2, 3, 1, 0)
LAST = (8,)


def below(s):
    return 2 * s - 1 if s else 0


def above(s):
    return 2 * s


def pair(s):
    if s == 0:
        return 0, 1
    return (2 * s - 1, 2) if s < FAR else (2 * FAR - 1, 1)


def join(v):
    lane = lax.broadcasted_iota(jnp.int32, (1, LANES), 1)
    middle = (lane >= ROWS) & (lane < 2 * ROWS)
    rows = [v[i] for i in range(v.shape[0])]
    top = rows[0]
    for r in rows[1:]:
        top = jnp.maximum(top, r)
    total = jnp.zeros_like(top)
    for r in rows:
        scale = pltpu.roll(jnp.exp(r - top), ROWS, 1)
        total = total + r * jnp.where(middle, scale, 1.0)
    return jnp.where(lane < ROWS, top, total)


def kernel(hidden, weight, shares, targets, out,
           X, W, acc, part, spare, goal, own_sh, pack, sxy, sz,
           out_sem, zr, ar, rr, orr, vr, fr, ws, wr, wl, hl, gl, ps, pr,
           xs, xr, ts, tr):
    pipe = lax.axis_index("pipe")
    tensor = lax.axis_index("tensor")
    x, y = pipe // NY, pipe % NY
    z, c = tensor // 2, tensor % 2

    def at_xy(dx, dy):
        return (((x + dx) % NX) * NY + (y + dy) % NY, tensor)

    def at_z(d):
        return (pipe, ((z + d) % NZ) * 2 + c)

    sibling = (pipe, z * 2 + 1 - c)
    sent = []

    def send(src, dst, recv_sem, device):
        pltpu.make_async_remote_copy(
            src_ref=src, dst_ref=dst, send_sem=out_sem, recv_sem=recv_sem,
            device_id=device, device_id_type=MESH).start()
        sent.append(math.prod(src.shape))

    def arrived(ref, sem):
        pltpu.make_async_copy(ref, ref, sem).wait()

    def feature_block(j, core):
        step = (j + 1) // 2
        at = jnp.where(j % 2 == 1, z + NZ - step, z + step) % NZ
        return pl.ds(pl.multiple_of((2 * at + core) * WIDTH, WIDTH), WIDTH)

    def own_weight(j):
        return pltpu.make_async_copy(
            weight.at[:, feature_block(j, c)], W.at[j, pl.ds(0, SLOTS), :], wl)

    def other_weight(j):
        return pltpu.make_async_remote_copy(
            src_ref=weight.at[:, feature_block(j, 1 - c)],
            dst_ref=W.at[j, pl.ds(SLOTS, SLOTS), :],
            send_sem=ws, recv_sem=wr, device_id=sibling, device_id_type=MESH)

    barrier = pltpu.get_barrier_semaphore()
    greet = [at_xy(1, 0), at_xy(3, 0), at_xy(0, 1), at_xy(0, 3), at_z(1), at_z(15),
             at_xy(2, 0), at_xy(0, 2), sibling]
    for device in greet:
        pl.semaphore_signal(barrier, inc=1, device_id=device, device_id_type=MESH)
    own_block = pltpu.make_async_copy(hidden, X.at[0, 0, 0], hl)
    own_block.start()
    pl.semaphore_wait(barrier, len(greet))

    wide, narrow = pl.ds(0, WIDE), pl.ds(WIDE, WIDTH - WIDE)
    upper, lower = pl.ds(0, HALF), pl.ds(HALF, HALF)
    both = pl.ds(0, ROWS)

    def z_send(s):
        hop = HOP[s - 1]
        if s == hop:
            src_up = src_down = hidden.at[:, wide]
        else:
            src_up, src_down = X.at[below(s - hop), 0, 0, :, wide], X.at[above(s - hop), 0, 0, :, wide]
        dst_up, dst_down = X.at[below(s), 0, 0, :, wide], X.at[min(above(s), NZ - 1), 0, 0, :, wide]
        if s == FAR:
            src_up, dst_up = src_up.at[upper], dst_up.at[upper]
            src_down, dst_down = src_down.at[lower], dst_down.at[lower]
        send(src_up, dst_up, zr.at[s - 1], at_z(hop))
        send(src_down, dst_down, zr.at[s - 1], at_z(NZ - hop))

    def blocks(n):
        return X.at[pl.ds(0, n), 0, 0, :, wide]

    def strips(a, b):
        return X.at[0, pl.ds(0, a), pl.ds(0, b), :, narrow]

    def z_wait(s):
        arrived(blocks(2 if s < FAR else 1), zr.at[s - 1])

    def o_send(s):
        first, n = pair(s)
        at = pl.ds(first, n)
        if s == 0:
            def src(r):
                return hidden.at[r, wide]

            def dst(a, b, r):
                return X.at[0, a, b, r, wide]
        else:
            def src(r):
                return X.at[at, 0, 0, r, wide]

            def dst(a, b, r):
                return X.at[at, a, b, r, wide]
        plan = [((1, 0), both), ((0, 1), both), ((3, 0), both), ((0, 3), both), ((2, 0), upper), ((0, 2), lower)]
        for (dx, dy), r in plan:
            send(src(r), dst(-dx % NX, -dy % NY, r), orr.at[s], at_xy(dx, dy))

    def o_wait(s):
        arrived(blocks(5 * pair(s)[1]), orr.at[s])

    def v_send(s):
        at, rest = pl.ds(*pair(s)), pl.ds(1, 3)
        for d in (1, 3):
            send(X.at[at, rest, 0, upper, wide], X.at[at, rest, -d % NY, upper, wide],
                 vr.at[s], at_xy(0, d))
            send(X.at[at, 0, rest, lower, wide], X.at[at, -d % NX, rest, lower, wide],
                 vr.at[s], at_xy(d, 0))

    def v_wait(s):
        arrived(blocks(6 * pair(s)[1]), vr.at[s])

    def f_send(s):
        at = pl.ds(*pair(s))
        for i, d in enumerate((1, 3)):
            h = pl.ds(2 * i, 2)
            send(X.at[at, h, -d % NY, upper, wide], X.at[at, h, 2, upper, wide],
                 fr.at[s], at_xy(0, d))
            send(X.at[at, -d % NX, h, lower, wide], X.at[at, 2, h, lower, wide],
                 fr.at[s], at_xy(d, 0))

    def f_wait(s):
        arrived(blocks(4 * pair(s)[1]), fr.at[s])

    def a1_send():
        for d in (1, 3, 2):
            send(hidden.at[:, narrow], X.at[0, -d % NX, 0, :, narrow], ar.at[1], at_xy(d, 0))

    def a0_send():
        for d in (1, 3, 2):
            send(hidden.at[:, narrow], X.at[0, 0, -d % NY, :, narrow], ar.at[0], at_xy(0, d))

    def a0_wait():
        arrived(strips(1, 3), ar.at[0])

    def a2_send():
        arrived(strips(1, 3), ar.at[1])
        rest = pl.ds(1, 3)
        for d in (1, 3, 2):
            send(X.at[0, rest, 0, :, narrow], X.at[0, rest, -d % NY, :, narrow], ar.at[2], at_xy(0, d))

    def a2_wait():
        arrived(strips(3, 3), ar.at[2])

    def slab(j, h):
        if PIECES == NX:
            return X.at[j, pl.ds(h, 1), :, :, narrow]
        return X.at[j, pl.ds(h // 2, 1), pl.ds(2 * (h % 2), 2), :, narrow]

    def ring_send(s, h):
        if s < FAR or h < PIECES // 2:
            send(slab(below(s - 1), h), slab(below(s), h), rr.at[s - 1, h], at_z(1))
        if s < FAR or h >= PIECES // 2:
            send(slab(above(s - 1), h), slab(min(above(s), NZ - 1), h), rr.at[s - 1, h], at_z(NZ - 1))

    def ring_wait(s, h):
        n = NX * NY // PIECES * (2 if s < FAR else 1)
        arrived(strips(n // min(n, NY), min(n, NY)), rr.at[s - 1, h])

    def row_send(src, dst, send_sem, recv_sem, device):
        pltpu.make_async_remote_copy(
            src_ref=src, dst_ref=dst, send_sem=send_sem, recv_sem=recv_sem,
            device_id=device, device_id_type=MESH).start()

    def swap(dx):
        cols = pl.ds(dx * LANES, LANES)
        return pltpu.make_async_remote_copy(
            src_ref=acc.at[pl.ds(SLOTS, SLOTS), cols], dst_ref=part.at[:, cols],
            send_sem=ps, recv_sem=pr.at[dx], device_id=sibling, device_id_type=MESH)

    def multiply_last():
        first, n = pair(LAST[0])[0], sum(pair(s)[1] for s in LAST)

        def add(slots, x0):
            cols = pl.ds(x0 * LANES, 2 * LANES)
            total = acc[slots, cols]
            for j in range(first, first + n):
                total += lax.dot_general(
                    W[j, slots, :], X[j, pl.ds(x0, 2)].reshape(2 * NY * ROWS, WIDTH),
                    (((1,), (1,)), ((), ())), preferred_element_type=jnp.float32)
            acc[slots, cols] = total

        for x0 in (2, 0):
            add(pl.ds(SLOTS, SLOTS), x0)
            for dx in DXS:
                if dx // 2 == x0 // 2:
                    swap(dx).start()
        for x0 in (2, 0):
            add(pl.ds(0, SLOTS), x0)

    def multiply(s):
        first, n = pair(s)
        if s == 0:
            arrived(W.at[:, pl.ds(0, SLOTS), :], wl)
            arrived(W.at[:, pl.ds(SLOTS, SLOTS), :], wr)

        @pl.loop(first, first + n)
        def _(j):
            part_sum = lax.dot_general(
                W[j], X[j].reshape(NX * NY * ROWS, WIDTH),
                (((1,), (1,)), ((), ())), preferred_element_type=jnp.float32)
            if s == 0:
                acc[...] = part_sum
            else:
                acc[...] += part_sum

    def all_left():
        assert sum(sent) == math.prod(X.shape) - ROWS * WIDTH
        arrived(X, out_sem)
        arrived(W.at[:, pl.ds(SLOTS, SLOTS), :], ws)

    for t in range(1, FAR + 1):
        if t == HOP[t - 1]:
            z_send(t)
    o_send(0)
    a1_send()
    a0_send()

    @pl.loop(0, NZ)
    def _(j):
        other_weight(j).start()
        own_weight(j).start()

    goals = [pltpu.make_async_copy(targets.at[(x + d) % NX], goal.at[d], gl.at[0]) for d in range(NX)]
    share_copy = pltpu.make_async_copy(shares, own_sh, gl.at[1])
    for g in goals + [share_copy]:
        g.start()
    pltpu.make_async_copy(hidden, spare, out_sem).start()

    known = {}

    def prepare():
        arrived(goal, gl.at[0])
        share_copy.wait()
        own_share = jnp.int32(0)
        offset = jnp.int32(0)
        for s in range(NX * NY):
            own_share = own_share + jnp.where(s == pipe, own_sh[s], 0)
            offset = offset + jnp.where(s < pipe, own_sh[s], 0)
        known["share"] = own_share
        for dx in range(NX):
            want = goal[dx] - offset
            turned = want
            for k in range(1, NY):
                turned = jnp.where(y == k, pltpu.roll(want, LANES - ROWS * k, 1), turned)
            goal[dx] = turned

    def event(kind, s=0, h=0):
        if kind == "z":
            z_wait(s)
            for t in range(s + 1, FAR + 1):
                if t - HOP[t - 1] == s:
                    z_send(t)
            o_send(s)
        elif kind == "o":
            o_wait(s)
            v_send(s)
        elif kind == "v":
            v_wait(s)
            f_send(s)
        elif kind == "m":
            f_wait(s)
            if s not in LAST:
                multiply(s)
        elif kind == "a0":
            a0_wait()
            for h in range(PIECES // NX):
                ring_send(1, h)
        elif kind == "a2":
            a2_send()
        elif kind == "a3":
            a2_wait()
            for h in range(PIECES // NX, PIECES):
                ring_send(1, h)
        else:
            ring_wait(s, h)
            if s < FAR:
                ring_send(s + 1, h)

    own_block.wait()
    for name in ORDER:
        event(*name)
        if name == ("m", 0):
            prepare()
    multiply_last()

    lane = lax.broadcasted_iota(jnp.int32, (1, LANES), 1)

    def packed(values, dy):
        top, total, pick = values
        moved = [pltpu.roll(v, (ROWS * (i - dy)) % LANES, 1) if (ROWS * (i - dy)) % LANES else v
                 for i, v in enumerate((top, total, pick))]
        return jnp.where(lane < ROWS, moved[0], jnp.where(lane < 2 * ROWS, moved[1], moved[2]))

    position = lax.broadcasted_iota(jnp.int32, (SLOTS, LANES), 0) * (2 * NZ) + tensor
    live = position < known["share"]
    for dx in DXS:
        cols = pl.ds(dx * LANES, LANES)
        swap(dx).wait_recv()
        logits = acc[pl.ds(0, SLOTS), cols] + part[:, cols]
        top = jnp.max(jnp.where(live, logits, VERY_NEGATIVE), axis=0, keepdims=True)
        total = jnp.sum(jnp.where(live, jnp.exp(logits - top), 0.0), axis=0, keepdims=True)
        pick = jnp.sum(jnp.where(live & (position == goal[dx]), logits, 0.0), axis=0, keepdims=True)
        for dy in DXS:
            row = packed((top, total, pick), dy)
            to = c * NX * NY + (-dx % NX) * NY + (-dy % NY)
            if dx == 0 and dy == 0:
                sxy[to] = row
                row_send(sxy.at[to], sxy.at[to], xs, xr, sibling)
            else:
                pack[dx * NY + dy] = row
                for core in range(2):
                    device = (at_xy(dx, dy)[0], z * 2 + core)
                    row_send(pack.at[dx * NY + dy], sxy.at[to], xs, xr, device)
    arrived(sxy.at[pl.ds(1, 2 * NX * NY - 1)], xr)
    sz[z] = join(sxy[...])
    for d in (8, 7, 9, 6, 10, 5, 11, 4, 12, 3, 13, 2, 14, 1, 15):
        row_send(sz.at[z], sz.at[z], ts, tr, at_z(d))
    arrived(part, ps)
    all_left()
    arrived(sz.at[pl.ds(1, NZ - 1)], tr)
    row = join(sz[...])
    log_total = pltpu.roll(row, ROWS, 1) + jnp.log(jnp.where((lane >= ROWS) & (lane < 2 * ROWS), row, 1.0))
    out[...] = jnp.where(lane < ROWS, row, jnp.where(
        lane < 2 * ROWS, log_total, row - pltpu.roll(log_total, ROWS, 1)))
    arrived(sxy.at[pl.ds(1, 2 * NX * NY - 1)], xs)
    arrived(sz.at[pl.ds(1, NZ - 1)], ts)


def local(hidden, head_weight, shares, targets):
    dma = pltpu.SemaphoreType.DMA
    rows = NX * NY * ROWS
    n = FAR + 1
    line = lambda k: pltpu.VMEM((k, 1, LANES), jnp.float32)
    hbm = pl.BlockSpec(memory_space=pltpu.HBM)
    out = pl.pallas_call(
        kernel,
        out_shape=jax.ShapeDtypeStruct((1, LANES), jnp.float32),
        in_specs=[hbm] * 4,
        out_specs=pl.BlockSpec(memory_space=pltpu.VMEM),
        scratch_shapes=[
            pltpu.VMEM((NZ, NX, NY, ROWS, WIDTH), jnp.bfloat16),
            pltpu.VMEM((NZ, 2 * SLOTS, WIDTH), jnp.bfloat16),
            pltpu.VMEM((2 * SLOTS, rows), jnp.float32),
            pltpu.VMEM((SLOTS, rows), jnp.float32),
            pltpu.VMEM((ROWS, WIDTH), jnp.bfloat16),
            pltpu.VMEM((NX, 1, LANES), jnp.int32),
            pltpu.SMEM((NX * NY,), jnp.int32),
            line(NX * NY), line(2 * NX * NY), line(NZ),
            dma(()), dma((FAR,)), dma((3,)), dma((FAR, PIECES)), dma((n,)), dma((n,)), dma((n,)),
            dma(()), dma(()), dma(()), dma(()), dma((2,)), dma(()), dma((NX,)),
            *[dma(()) for _ in range(4)],
        ],
        compiler_params=pltpu.CompilerParams(
            collective_id=0, has_side_effects=True, vmem_limit_bytes=60 * 1024 * 1024),
        cost_estimate=pl.CostEstimate(
            flops=2 * rows * SLOTS * 2 * NZ * WIDTH, bytes_accessed=22 * 1024 * 1024,
            transcendentals=rows * SLOTS),
    )(hidden, head_weight, shares, targets.reshape(NX, 1, LANES))
    return tuple(out[0, ROWS * i:ROWS * (i + 1)] for i in range(3))


def solution(mesh):
    in_specs = (P("pipe", "tensor"), P(("pipe", "tensor"), None), P(), P())
    out_specs = (P("pipe"), P("pipe"), P("pipe"))
    return jax.shard_map(local, mesh=mesh, in_specs=in_specs, out_specs=out_specs, check_vma=False)
```
